128 devices in a mesh: context: 8 (over z_lo, y), expert: 16 (over z_hi, x, core).
Axes of the slice: x: 4, y: 4, z: 4 (z_hi: 2, z_lo: 2; z = z_hi * 2 + z_lo), core: 2. Of those that a mesh axis runs over, the one named last changes fastest.
Arguments:
- queries: bfloat16 [2, 1024, 4096], P(None, 'context', 'expert'), may hold values from -5 to 5
- keys: bfloat16 [2, 1024, 512], P(None, 'context'), may hold values from -5 to 5
- values: bfloat16 [2, 1024, 512], P(None, 'context'), may hold values from -8 to 8
- out_proj: bfloat16 [4096, 4096], P('expert'), may hold values from -0.09375 to 0.09375
- residual: bfloat16 [2, 1024, 4096], P(None, ('context', 'expert')), may hold values from -9 to 9
- norm_gain: float32 [4096], replicated, may hold values from 0.25 to 1.75
- w_in: bfloat16 [128, 4096, 1536], P(('context', 'expert')), may hold values from -0.09375 to 0.09375
- w_out: bfloat16 [128, 768, 4096], P(('context', 'expert')), may hold values from -0.15625 to 0.15625
- expert_ids: int32 [2, 1024, 8], P(None, ('context', 'expert')), may hold values from 0 to 63, as said below
- gate_weights: float32 [2, 1024, 8], P(None, ('context', 'expert')), may hold values from 0.02 to 0.25
Outputs:
- out: bfloat16 [2, 1024, 4096], P(None, ('context', 'expert'))
The draws below stay inside these ranges and needn't reach their ends.
Inputs may be any that keep to these rules, and one draw needn't show every extreme that they name: `expert_ids`: each row names 8 different experts. In each micro-batch the 8 rows of one device (aligned blocks along the sequence) name no expert more than 2 times, and one expert is named exactly 2 times in every such block.
All inputs are finite; a program needn't handle non-finite values.
Results may differ from the reference program's by a relative error of at most 0.02.
Values may be sent and summed in bfloat16 or wider, within the bound.
No kernel may reach another device: no remote copies, remote signals or barrier semaphores. Data moves between devices by JAX's collectives and lax.ppermute only.
A program may use at most 128 MiB of HBM per device.

```python
import math
import jax
import jax.numpy as jnp
from jax import lax

D = 4096
QH = 32
KVH = 4
HD = 128
FF = 1536
TOPK = 8
MB = 2
BLOCK = 64
HF = 768
EXPERTS = 64
SEQ = 1024
MOE_ROWS = 8
CAP = 2
N_CONTEXT = 8
N_EXPERT = 16


def draw_queries(key, part):
    key = jax.random.fold_in(key, 11)
    return jnp.clip(1.4 * jax.random.normal(key, (MB, SEQ, QH * HD)), -5.0, 5.0).astype(jnp.bfloat16)


def draw_keys(key, part):
    key = jax.random.fold_in(key, 12)
    return jnp.clip(1.4 * jax.random.normal(key, (MB, SEQ, KVH * HD)), -5.0, 5.0).astype(jnp.bfloat16)


def draw_residual(key, part):
    key = jax.random.fold_in(key, 31)
    noise_key = jax.random.fold_in(key, 1)
    row_key = jax.random.fold_in(key, 2)
    column_key = jax.random.fold_in(key, 3)
    base_values = jnp.clip(jax.random.normal(noise_key, (MB, SEQ, D)), -3.0, 3.0)
    row_scale = jnp.exp(jax.random.uniform(row_key, (MB, SEQ, 1), minval=math.log(0.2), maxval=math.log(2.0)))
    column_scale = jnp.exp(jax.random.uniform(column_key, (1, 1, D), minval=math.log(0.3), maxval=math.log(1.5)))
    return (base_values * row_scale * column_scale).astype(jnp.bfloat16)


def draw_expert_ids(key, part):
    key = jax.random.fold_in(key, 21)
    block_count = SEQ // MOE_ROWS
    base_count = TOPK * MOE_ROWS // EXPERTS
    hot_expert = jax.random.randint(jax.random.fold_in(key, 1), (MB,), 0, EXPERTS)

    def one_block(block_key, hot_one):
        order_key = jax.random.fold_in(block_key, 1)
        spread_key = jax.random.fold_in(block_key, 2)
        shuffle_key = jax.random.fold_in(block_key, 3)
        ranking = jax.random.permutation(order_key, EXPERTS).astype(jnp.int32)
        ranking = jnp.where(ranking == hot_one, ranking[0], ranking).at[0].set(hot_one)
        spread = jax.random.randint(spread_key, (EXPERTS // 2,), 0, base_count + 1).at[0].set(base_count)
        counts = jnp.stack([base_count + spread, base_count - spread], axis=1).reshape(EXPERTS)
        count_ends = jnp.cumsum(counts)
        places = jnp.arange(TOPK * MOE_ROWS, dtype=jnp.int32)
        rank_index = jnp.sum((count_ends[None, :] <= places[:, None]).astype(jnp.int32), axis=1)
        id_table = ranking[rank_index].reshape(TOPK, MOE_ROWS).T
        return id_table[jax.random.permutation(shuffle_key, MOE_ROWS)]

    def one_batch(batch_index):
        batch_key = jax.random.fold_in(key, 100 + batch_index)

        def by_block(block_index):
            return one_block(jax.random.fold_in(batch_key, block_index), hot_expert[batch_index])
        return jax.vmap(by_block)(jnp.arange(block_count, dtype=jnp.int32))
    drawn = jax.vmap(one_batch)(jnp.arange(MB, dtype=jnp.int32))
    return drawn.reshape(MB, SEQ, TOPK).astype(jnp.int32)


def block_scale(own_key, dims, split, smallest, high):
    gain, own = 1.0, jax.random.fold_in(own_key, 6)
    for axis_at, parts in split:
        draws = jnp.exp(jax.random.uniform(jax.random.fold_in(own, axis_at), (parts,), jnp.float32, smallest / len(split), high / len(split)))
        gain = gain * jnp.repeat(draws, dims[axis_at] // parts).reshape([-1 if axis == axis_at else 1 for axis in range(len(dims))])
    return gain


def bell_draw(key, extent, deviation, limit, split=(), kind=jnp.bfloat16):
    level = block_scale(key, extent, split, -0.22, 0.18) if split else 1.0
    entries = jax.random.normal(key, extent, jnp.float32) * deviation * level
    return jnp.minimum(jnp.maximum(entries, -limit), limit).astype(kind)


def setup_inputs(seed: int = 0) -> dict:
    key_of = jax.random.split(jax.random.key(seed), 11)
    return {
        "queries": draw_queries(jax.random.fold_in(key_of[10], 71), 0),
        "keys": draw_keys(jax.random.fold_in(key_of[10], 71), 0),
        "values": bell_draw(key_of[2], (MB, SEQ, KVH * HD), 1.5, 8.0, ((1, 8),)),
        "out_proj": bell_draw(key_of[3], (QH * HD, D), (QH * HD) ** -0.5, 0.09375, ((0, 16),)),
        "residual": draw_residual(jax.random.fold_in(key_of[10], 71), 0),
        "norm_gain": jnp.clip(1.0 + 0.15 * jax.random.normal(key_of[5], (D,), jnp.float32), 0.25, 1.75),
        "w_in": bell_draw(key_of[6], (2 * EXPERTS, D, FF), D ** -0.5, 0.09375, ((0, 128),)),
        "w_out": bell_draw(key_of[7], (2 * EXPERTS, HF, D), FF ** -0.5, 0.15625, ((0, 128),)),
        "expert_ids": draw_expert_ids(jax.random.fold_in(key_of[10], 71), 0),
        "gate_weights": jnp.clip(0.02 + 0.23 * jax.random.uniform(key_of[9], (MB, SEQ, TOPK), jnp.float32) ** block_scale(key_of[9], (MB, SEQ, TOPK), ((1, 128),), -0.2, 0.2), 0.02, 0.25),
    }


masked_score = -1e+30

def folded_positions(row_count):
    stored = jnp.arange(row_count, dtype=jnp.int32)
    block_index = stored // BLOCK
    block_order = jnp.where(block_index % 2 == 0, block_index // 2, 2 * N_CONTEXT - 1 - block_index // 2)
    return block_order * BLOCK + stored % BLOCK

def attention(query_rows, key_rows, value_rows):
    position = folded_positions(SEQ)
    allowed = position[None, :] <= position[:, None]
    query_heads = query_rows.reshape(SEQ, QH, HD).transpose(1, 0, 2)
    key_heads = key_rows.reshape(SEQ, KVH, HD).transpose(1, 0, 2)
    value_heads = value_rows.reshape(SEQ, KVH, HD).transpose(1, 0, 2)
    group_size = QH // KVH

    def one_head(operands):
        query_head, head_index = operands
        key_head = key_heads[head_index // group_size]
        value_head = value_heads[head_index // group_size]
        scores = jnp.dot(query_head, key_head.T, preferred_element_type=jnp.float32) * HD ** (-0.5)
        scores = jnp.where(allowed, scores, masked_score)
        largest = lax.optimization_barrier(jnp.max(scores, axis=-1, keepdims=True))
        weights = jnp.where(allowed, jnp.exp(scores - largest), 0.0)
        probabilities = (weights / lax.optimization_barrier(jnp.sum(weights, axis=-1, keepdims=True))).astype(jnp.bfloat16)
        return jnp.dot(probabilities, value_head, preferred_element_type=jnp.float32)
    outputs = lax.map(one_head, (query_heads, jnp.arange(QH, dtype=jnp.int32)))
    return outputs.transpose(1, 0, 2).reshape(SEQ, QH * HD).astype(jnp.bfloat16)

def expert_half(row_block, in_weights, out_weights):
    mixed = jnp.dot(row_block, in_weights, preferred_element_type=jnp.float32)
    hidden = (jax.nn.silu(mixed[:, :HF]) * mixed[:, HF:]).astype(jnp.bfloat16)
    partial_value = jnp.dot(hidden, out_weights, preferred_element_type=jnp.float32).astype(jnp.bfloat16)
    return lax.optimization_barrier(partial_value).astype(jnp.float32)

def experts_for(normed, id_rows, gate_rows, w_in, w_out):
    block_count = SEQ // MOE_ROWS
    pick_count = MOE_ROWS * TOPK
    id_blocks = id_rows.reshape(block_count, pick_count)
    onehot = (id_blocks[:, :, None] == jnp.arange(EXPERTS, dtype=jnp.int32)[None, None, :]).astype(jnp.int32)
    slot_index = lax.optimization_barrier(jnp.sum((jnp.cumsum(onehot, axis=1) - onehot) * onehot, axis=2)).astype(jnp.int32)
    block_rows = jnp.arange(block_count, dtype=jnp.int32)[:, None]
    token_index = block_rows * MOE_ROWS + jnp.arange(pick_count, dtype=jnp.int32)[None, :] // TOPK
    id_table = jnp.full((EXPERTS, block_count, CAP), SEQ, dtype=jnp.int32)
    id_table = id_table.at[id_blocks, block_rows, slot_index].set(token_index)
    padded = jnp.concatenate([normed, jnp.zeros((1, D), normed.dtype)], axis=0)
    in_grid = w_in.reshape(N_CONTEXT // 2, 2, N_EXPERT, D, FF)
    out_grid = w_out.reshape(N_CONTEXT // 2, 2, N_EXPERT, HF, D)

    def one_expert(expert):
        row_block = padded[id_table[expert].reshape(-1)]
        pair_index = expert // N_EXPERT
        column = expert % N_EXPERT
        expert_sum = expert_half(row_block, in_grid[pair_index, 0, column], out_grid[pair_index, 0, column])
        expert_sum = expert_sum + expert_half(row_block, in_grid[pair_index, 1, column], out_grid[pair_index, 1, column])
        return expert_sum.astype(jnp.bfloat16)
    outputs = lax.map(one_expert, jnp.arange(EXPERTS, dtype=jnp.int32))
    picked = outputs[id_blocks, block_rows * CAP + slot_index].astype(jnp.float32)
    picked = picked.reshape(SEQ, TOPK, D)
    return lax.optimization_barrier(jnp.sum(picked * gate_rows[:, :, None], axis=1))

def reference(queries, keys, values, out_proj, residual, norm_gain, w_in, w_out, expert_ids, gate_weights):
    results = []
    for batch_index in range(MB):
        attended = attention(queries[batch_index], keys[batch_index], values[batch_index])
        residual_sum = residual[batch_index].astype(jnp.float32) + jnp.dot(attended, out_proj, preferred_element_type=jnp.float32)
        scale_rows = lax.rsqrt(lax.optimization_barrier(jnp.mean(residual_sum * residual_sum, axis=-1, keepdims=True)) + 1e-06)
        normed = (residual_sum * scale_rows * norm_gain).astype(jnp.bfloat16)
        mixed = experts_for(normed, expert_ids[batch_index], gate_weights[batch_index], w_in, w_out)
        results.append((residual_sum + mixed).astype(jnp.bfloat16))
    return jnp.stack(results)
```

```python
import jax
import jax.numpy as jnp
from jax import lax
from jax.sharding import Mesh, PartitionSpec as P

QH = 32
KVH = 4
HD = 128
BLOCK = 64
masked_score = -1e30

CONTEXT = ("zl", "y")
COLUMN = ("zh", "x")
CHIPS = ("zl", "y", "zh", "x")
SWAP = [(0, 1), (1, 0)]


def swap_cores(value):
    return lax.ppermute(value, "core", SWAP)


def folded_positions(first_row, row_count, context_size):
    stored = first_row + jnp.arange(row_count, dtype=jnp.int32)
    block_index = stored // BLOCK
    block_order = jnp.where(
        block_index % 2 == 0, block_index // 2, 2 * context_size - 1 - block_index // 2
    )
    return block_order * BLOCK + stored % BLOCK


def attend(query_heads, keys, values, query_position, key_position):
    allowed = (key_position[None, :] <= query_position[:, None])[None]
    scores = jnp.einsum(
        "hqd,kd->hqk", query_heads, keys, preferred_element_type=jnp.float32
    ) * HD ** (-0.5)
    scores = jnp.where(allowed, scores, masked_score)
    largest = jnp.max(scores, axis=-1, keepdims=True)
    weights = jnp.exp(scores - largest)
    total = jnp.sum(weights, axis=-1, keepdims=True)
    weighted = jnp.einsum(
        "hqk,kd->qhd", weights.astype(jnp.bfloat16), values, preferred_element_type=jnp.float32
    )
    return (weighted / total.transpose(1, 0, 2)).astype(jnp.bfloat16)


def local(
    queries, keys, values, out_proj, residual, norm_gain, w_in, w_out, expert_ids, gate_weights
):
    batch_count, row_count, feature_count = queries.shape
    token_rows, top_count = expert_ids.shape[1:]
    model_width = out_proj.shape[1]
    context_size = lax.axis_size(CONTEXT)
    column_size = lax.axis_size(COLUMN)
    chip_count = context_size * column_size
    core = lax.axis_index("core")
    heads_here = feature_count // HD
    chip_rows = 2 * token_rows

    def of_batch(value, index):
        return lax.dynamic_index_in_dim(value, index, 0, keepdims=False)

    other_queries = swap_cores(of_batch(queries, 1 - core))
    other_proj = swap_cores(out_proj)
    other_residual = swap_cores(of_batch(residual, 1 - core))
    other_ids = swap_cores(expert_ids)
    other_gates = swap_cores(gate_weights)

    def in_core_order(own, other, axis):
        stacked = jnp.stack([own, other], axis=axis)
        flipped = jnp.stack([other, own], axis=axis)
        return jnp.where(core == 0, stacked, flipped)

    kv_head = lax.axis_index(COLUMN) * 2 * heads_here // (QH // KVH)
    pair = jnp.stack([of_batch(keys, core), of_batch(values, core)])
    pair = lax.dynamic_slice_in_dim(pair, kv_head * HD, HD, 2)
    gathered = lax.all_to_all(
        jnp.broadcast_to(pair[None], (context_size,) + pair.shape), CONTEXT, 0, 0
    )
    all_keys = gathered[:, 0].reshape(context_size * row_count, HD)
    all_values = gathered[:, 1].reshape(context_size * row_count, HD)
    query_rows = jnp.concatenate([of_batch(queries, core), other_queries], axis=1)
    query_heads = query_rows.reshape(row_count, 2 * heads_here, HD).transpose(1, 0, 2)
    attended = attend(
        query_heads,
        all_keys,
        all_values,
        folded_positions(lax.axis_index(CONTEXT) * row_count, row_count, context_size),
        folded_positions(0, context_size * row_count, context_size),
    ).reshape(row_count, 2 * feature_count)
    projected = jnp.dot(
        attended,
        jnp.concatenate([out_proj, other_proj], axis=0),
        preferred_element_type=jnp.float32,
    ).astype(jnp.bfloat16)
    pieces = lax.all_to_all(
        projected.reshape(column_size, chip_rows, model_width), COLUMN, 0, 0
    )
    residual_rows = in_core_order(of_batch(residual, core), other_residual, 0)
    residual_sum = residual_rows.reshape(chip_rows, model_width).astype(jnp.float32) + jnp.sum(
        pieces.astype(jnp.float32), axis=0
    )
    scale_rows = lax.rsqrt(jnp.mean(residual_sum * residual_sum, axis=-1, keepdims=True) + 1e-06)
    normed = (residual_sum * scale_rows * norm_gain).astype(jnp.bfloat16)
    tokens = batch_count * chip_rows
    all_normed = in_core_order(normed, swap_cores(normed), 0).reshape(tokens, model_width)

    ids = in_core_order(expert_ids, other_ids, 1)
    gates = in_core_order(gate_weights, other_gates, 1).reshape(tokens, top_count)
    experts_total = chip_count
    onehot = (
        ids.reshape(batch_count * 2, token_rows * top_count)[:, :, None]
        == jnp.arange(experts_total, dtype=jnp.int32)
    ).astype(jnp.int32)
    slot_index = jnp.sum((jnp.cumsum(onehot, axis=1) - onehot) * onehot, axis=2)
    flat = ids.reshape(batch_count * 2, token_rows * top_count)
    block_index = jnp.arange(batch_count * 2, dtype=jnp.int32)[:, None]
    slots = batch_count * 2 * 2
    target = jnp.where(
        flat % 2 == core, (flat // 2) * slots + block_index * 2 + slot_index, -1
    ).reshape(tokens, top_count)
    slot_rows = experts_total // 2 * slots
    matches = target[None] == jnp.arange(slot_rows, dtype=jnp.int32)[:, None, None]
    gate_matrix = jnp.sum(jnp.where(matches, gates[None], 0.0), axis=2)
    placing = jnp.any(matches, axis=2).astype(jnp.bfloat16)

    def both_halves(matrix):
        grouped = matrix.reshape(context_size // 2, 1, slot_rows // (context_size // 2), tokens)
        return jnp.broadcast_to(
            grouped, (grouped.shape[0], 2, grouped.shape[2], tokens)
        ).reshape(2 * slot_rows, tokens)

    outgoing = jnp.dot(
        both_halves(placing), all_normed, preferred_element_type=jnp.float32
    ).astype(jnp.bfloat16)
    received = lax.all_to_all(
        outgoing.reshape(chip_count, slots, model_width), CHIPS, 0, 0
    ).reshape(chip_count * slots, model_width)
    mixed = jnp.dot(received, w_in[0], preferred_element_type=jnp.float32)
    half_width = w_out.shape[1]
    hidden = (jax.nn.silu(mixed[:, :half_width]) * mixed[:, half_width:]).astype(jnp.bfloat16)
    partial_value = jnp.dot(hidden, w_out[0], preferred_element_type=jnp.float32).astype(
        jnp.bfloat16
    )
    returned = lax.all_to_all(
        partial_value.reshape(chip_count, slots, model_width), CHIPS, 0, 0
    ).reshape(chip_count * slots, model_width)
    gate_high = gate_matrix.astype(jnp.bfloat16)
    gate_low = (gate_matrix - gate_high.astype(jnp.float32)).astype(jnp.bfloat16)
    both = jnp.concatenate([both_halves(gate_high), both_halves(gate_low)], axis=1)
    summed = lax.dot_general(
        both, returned, (((0,), (0,)), ((), ())), preferred_element_type=jnp.float32
    )
    mixed_out = (summed[:tokens] + summed[tokens:]).reshape(
        batch_count, 2, token_rows, model_width
    )
    own_sum = jnp.where(
        (jnp.arange(batch_count) == core)[:, None, None, None],
        residual_sum.reshape(1, 2, token_rows, model_width),
        0.0,
    )
    total = mixed_out + own_sum
    kept = lax.dynamic_index_in_dim(total, core, 1, keepdims=False)
    sent = lax.dynamic_index_in_dim(total, 1 - core, 1, keepdims=False)
    return (kept + swap_cores(sent)).astype(jnp.bfloat16)


def solution(mesh):
    chips = Mesh(mesh.devices.reshape(2, 4, 2, 4, 2), ("zl", "y", "zh", "x", "core"))
    expert = ("zh", "x", "core")
    every = CONTEXT + expert
    placed = (
        P(None, CONTEXT, expert),
        P(None, CONTEXT, None),
        P(None, CONTEXT, None),
        P(expert, None),
        P(None, every, None),
        P(),
        P(every, None, None),
        P(every, None, None),
        P(None, every, None),
        P(None, every, None),
    )
    return jax.shard_map(
        local,
        mesh=chips,
        in_specs=placed,
        out_specs=P(None, every, None),
        check_vma=False,
    )
```

```python
import functools

import jax
import jax.numpy as jnp
from jax import lax
from jax.experimental import pallas as pl
from jax.experimental.pallas import tpu as pltpu
from jax.sharding import Mesh, PartitionSpec as P

QH = 32
KVH = 4
HD = 128
BLOCK = 64
masked_score = -1e30

CONTEXT = ("zl", "y")
COLUMN = ("zh", "x")
CHIPS = ("zl", "y", "zh", "x")
SWAP = [(0, 1), (1, 0)]


def swap_cores(value):
    return lax.ppermute(value, "core", SWAP)


def folded(rows, piece, context_size):
    block_order = jnp.where(rows < BLOCK, piece, 2 * context_size - 1 - piece)
    return block_order * BLOCK + rows % BLOCK


def attention_kernel(
    index_ref, own_ref, other_ref, kv_ref, proj_ref, other_proj_ref, out_ref, proj, sems
):
    context_size, _, row_count, _ = kv_ref.shape
    feature_count = own_ref.shape[1]
    copies = [
        pltpu.make_async_copy(source, proj.at[pl.ds(part * feature_count, feature_count)], sems.at[part])
        for part, source in enumerate((proj_ref, other_proj_ref))
    ]
    for copy in copies:
        copy.start()
    key_count = context_size * row_count
    keys = kv_ref[:, 0].reshape(key_count, HD)
    values = kv_ref[:, 1].reshape(key_count, HD)
    query_rows = lax.broadcasted_iota(jnp.int32, (row_count, key_count), 0)
    key_rows = lax.broadcasted_iota(jnp.int32, (row_count, key_count), 1)
    allowed = folded(key_rows % row_count, key_rows // row_count, context_size) <= folded(
        query_rows, index_ref[0], context_size
    )
    heads = []
    for source in (own_ref, other_ref):
        for head in range(feature_count // HD):
            query = source[:, head * HD : (head + 1) * HD]
            scores = lax.dot_general(
                query, keys, (((1,), (1,)), ((), ())), preferred_element_type=jnp.float32
            ) * HD ** (-0.5)
            scores = jnp.where(allowed, scores, masked_score)
            weights = jnp.exp(scores - jnp.max(scores, axis=-1, keepdims=True))
            total = jnp.sum(weights, axis=-1, keepdims=True)
            weighted = jnp.dot(
                weights.astype(jnp.bfloat16), values, preferred_element_type=jnp.float32
            )
            heads.append((weighted / total).astype(jnp.bfloat16))
    attended = jnp.concatenate(heads, axis=1)
    for copy in copies:
        copy.wait()
    out_ref[...] = jnp.dot(attended, proj[...], preferred_element_type=jnp.float32).astype(
        jnp.bfloat16
    )


def attend(context_index, own, other, gathered, out_proj, other_proj):
    row_count, feature_count = own.shape
    model_width = out_proj.shape[1]
    whole = pl.BlockSpec(memory_space=pltpu.VMEM)
    apart = pl.BlockSpec(memory_space=pl.ANY)
    return pl.pallas_call(
        attention_kernel,
        in_specs=[pl.BlockSpec(memory_space=pltpu.SMEM), whole, whole, whole, apart, apart],
        out_specs=whole,
        out_shape=jax.ShapeDtypeStruct((row_count, model_width), jnp.bfloat16),
        scratch_shapes=[
            pltpu.VMEM((2 * feature_count, model_width), jnp.bfloat16),
            pltpu.SemaphoreType.DMA((2,)),
        ],
        compiler_params=pltpu.CompilerParams(vmem_limit_bytes=48 * 2**20),
    )(context_index, own, other, gathered, out_proj, other_proj)


def starts(sizes):
    return [sum(sizes[:part]) for part in range(len(sizes))]


def expert_kernel(
    rows_ref, w_in_ref, w_out_ref, out_ref,
    rows, w_in, w_out, mixed, hidden, result, row_sems, in_sems, out_sem, result_sems,
    *, depths, widths,
):
    half_width = w_out_ref.shape[0]
    pieces = list(zip(starts(depths), depths))
    row_copies = [
        pltpu.make_async_copy(
            rows_ref.at[:, pl.ds(first, size)], rows.at[:, pl.ds(first, size)], row_sems.at[part]
        )
        for part, (first, size) in enumerate(pieces)
    ]
    in_copies = [
        pltpu.make_async_copy(
            w_in_ref.at[pl.ds(first, size)], w_in.at[pl.ds(first, size)], in_sems.at[part]
        )
        for part, (first, size) in enumerate(pieces)
    ]
    out_copy = pltpu.make_async_copy(w_out_ref, w_out, out_sem)
    for part in range(len(pieces)):
        row_copies[part].start()
        in_copies[part].start()
    out_copy.start()
    for part, (first, size) in enumerate(pieces):
        row_copies[part].wait()
        in_copies[part].wait()
        product = jnp.dot(
            rows[:, first : first + size],
            w_in[first : first + size, :],
            preferred_element_type=jnp.float32,
        )
        if part == 0:
            mixed[...] = product
        elif part < len(pieces) - 1:
            mixed[...] += product
        else:
            total = mixed[...] + product
            gate = total[:, :half_width]
            hidden[...] = (gate / (1.0 + jnp.exp(-gate)) * total[:, half_width:]).astype(
                jnp.bfloat16
            )
    out_copy.wait()
    result_copies = []
    for part, (first, size) in enumerate(zip(starts(widths), widths)):
        columns = pl.ds(first, size)
        result[:, columns] = jnp.dot(
            hidden[...], w_out[:, columns], preferred_element_type=jnp.float32
        ).astype(jnp.bfloat16)
        copy = pltpu.make_async_copy(
            result.at[:, columns], out_ref.at[:, columns], result_sems.at[part]
        )
        copy.start()
        result_copies.append(copy)
    for copy in result_copies:
        copy.wait()


def expert_rows(rows, w_in, w_out):
    row_count, model_width = rows.shape
    half_width = w_out.shape[0]
    depths = tuple(model_width * part // 16 for part in (2, 4, 5, 5))
    widths = (model_width // 8,) * 8
    apart = pl.BlockSpec(memory_space=pl.ANY)
    return pl.pallas_call(
        functools.partial(expert_kernel, depths=depths, widths=widths),
        in_specs=[apart, apart, apart],
        out_specs=apart,
        out_shape=jax.ShapeDtypeStruct((row_count, model_width), jnp.bfloat16),
        scratch_shapes=[
            pltpu.VMEM((row_count, model_width), jnp.bfloat16),
            pltpu.VMEM((model_width, 2 * half_width), jnp.bfloat16),
            pltpu.VMEM((half_width, model_width), jnp.bfloat16),
            pltpu.VMEM((row_count, 2 * half_width), jnp.float32),
            pltpu.VMEM((row_count, half_width), jnp.bfloat16),
            pltpu.VMEM((row_count, model_width), jnp.bfloat16),
            pltpu.SemaphoreType.DMA((len(depths),)),
            pltpu.SemaphoreType.DMA((len(depths),)),
            pltpu.SemaphoreType.DMA,
            pltpu.SemaphoreType.DMA((len(widths),)),
        ],
        compiler_params=pltpu.CompilerParams(vmem_limit_bytes=52 * 2**20),
    )(rows, w_in, w_out)


def combine_kernel(gates_ref, returned_ref, base_ref, kept_ref, sent_ref):
    token_count = base_ref.shape[0]
    summed = jnp.dot(gates_ref[...], returned_ref[...], preferred_element_type=jnp.float32)
    total = summed[:token_count] + summed[token_count:] + base_ref[...]
    kept_ref[...] = total[: token_count // 2]
    sent_ref[...] = total[token_count // 2 :]


def combine(gates, returned, base):
    slot_count, model_width = returned.shape
    token_count = base.shape[0]
    width = model_width // 4
    half = jax.ShapeDtypeStruct((token_count // 2, model_width), jnp.float32)
    columns = lambda rows: pl.BlockSpec((rows, width), lambda step: (0, step))
    return pl.pallas_call(
        combine_kernel,
        grid=(model_width // width,),
        in_specs=[
            pl.BlockSpec(gates.shape, lambda step: (0, 0)),
            columns(slot_count),
            columns(token_count),
        ],
        out_specs=[columns(token_count // 2), columns(token_count // 2)],
        out_shape=[half, half],
        compiler_params=pltpu.CompilerParams(vmem_limit_bytes=32 * 2**20),
    )(gates, returned, base)


def local(
    queries, keys, values, out_proj, residual, norm_gain, w_in, w_out, expert_ids, gate_weights
):
    batch_count, row_count, feature_count = queries.shape
    token_rows, top_count = expert_ids.shape[1:]
    model_width = out_proj.shape[1]
    context_size = lax.axis_size(CONTEXT)
    column_size = lax.axis_size(COLUMN)
    chip_count = context_size * column_size
    core = lax.axis_index("core")
    heads_here = feature_count // HD
    chip_rows = 2 * token_rows

    def of_batch(value, index):
        return lax.dynamic_index_in_dim(value, index, 0, keepdims=False)

    other_queries = swap_cores(of_batch(queries, 1 - core))
    other_proj = swap_cores(out_proj)
    other_residual = swap_cores(of_batch(residual, 1 - core))
    other_ids = swap_cores(expert_ids)
    other_gates = swap_cores(gate_weights)

    def in_core_order(own, other, axis):
        stacked = jnp.stack([own, other], axis=axis)
        flipped = jnp.stack([other, own], axis=axis)
        return jnp.where(core == 0, stacked, flipped)

    kv_head = lax.axis_index(COLUMN) * 2 * heads_here // (QH // KVH)
    pair = jnp.stack([of_batch(keys, core), of_batch(values, core)])
    pair = lax.dynamic_slice_in_dim(pair, kv_head * HD, HD, 2)
    gathered = lax.all_to_all(
        jnp.broadcast_to(pair[None], (context_size,) + pair.shape), CONTEXT, 0, 0
    )
    projected = attend(
        lax.axis_index(CONTEXT).astype(jnp.int32).reshape(1),
        of_batch(queries, core),
        other_queries,
        gathered,
        out_proj,
        other_proj,
    )
    pieces = lax.all_to_all(
        projected.reshape(column_size, chip_rows, model_width), COLUMN, 0, 0
    )
    residual_rows = in_core_order(of_batch(residual, core), other_residual, 0)
    residual_sum = residual_rows.reshape(chip_rows, model_width).astype(jnp.float32) + jnp.sum(
        pieces.astype(jnp.float32), axis=0
    )
    scale_rows = lax.rsqrt(jnp.mean(residual_sum * residual_sum, axis=-1, keepdims=True) + 1e-06)
    normed = (residual_sum * scale_rows * norm_gain).astype(jnp.bfloat16)
    tokens = batch_count * chip_rows
    all_normed = in_core_order(normed, swap_cores(normed), 0).reshape(tokens, model_width)

    ids = in_core_order(expert_ids, other_ids, 1)
    gates = in_core_order(gate_weights, other_gates, 1).reshape(tokens, top_count)
    experts_total = chip_count
    onehot = (
        ids.reshape(batch_count * 2, token_rows * top_count)[:, :, None]
        == jnp.arange(experts_total, dtype=jnp.int32)
    ).astype(jnp.int32)
    slot_index = jnp.sum((jnp.cumsum(onehot, axis=1) - onehot) * onehot, axis=2)
    flat = ids.reshape(batch_count * 2, token_rows * top_count)
    block_index = jnp.arange(batch_count * 2, dtype=jnp.int32)[:, None]
    slots = batch_count * 2 * 2
    target = jnp.where(
        flat % 2 == core, (flat // 2) * slots + block_index * 2 + slot_index, -1
    ).reshape(tokens, top_count)
    slot_rows = experts_total // 2 * slots
    matches = target[None] == jnp.arange(slot_rows, dtype=jnp.int32)[:, None, None]
    gate_matrix = jnp.sum(jnp.where(matches, gates[None], 0.0), axis=2)
    placing = jnp.any(matches, axis=2).astype(jnp.bfloat16)

    def both_halves(matrix):
        grouped = matrix.reshape(context_size // 2, 1, slot_rows // (context_size // 2), tokens)
        return jnp.broadcast_to(
            grouped, (grouped.shape[0], 2, grouped.shape[2], tokens)
        ).reshape(2 * slot_rows, tokens)

    outgoing = jnp.dot(
        both_halves(placing), all_normed, preferred_element_type=jnp.float32
    ).astype(jnp.bfloat16)
    received = lax.all_to_all(
        outgoing.reshape(chip_count, slots, model_width), CHIPS, 0, 0
    ).reshape(chip_count * slots, model_width)
    partial_value = expert_rows(received, w_in[0], w_out[0])
    returned = lax.all_to_all(
        partial_value.reshape(chip_count, slots, model_width), CHIPS, 0, 0
    ).reshape(chip_count * slots, model_width)
    def kept_first(value):
        grouped = value.reshape((batch_count, 2, token_rows) + value.shape[1:])
        ordered = jnp.stack(
            [
                lax.dynamic_index_in_dim(grouped, core, 1, keepdims=False),
                lax.dynamic_index_in_dim(grouped, 1 - core, 1, keepdims=False),
            ]
        )
        return ordered.reshape(value.shape)

    gate_rows = kept_first(both_halves(gate_matrix).T)
    gate_high = gate_rows.astype(jnp.bfloat16)
    gate_low = (gate_rows - gate_high.astype(jnp.float32)).astype(jnp.bfloat16)
    own_sum = jnp.where(
        (jnp.arange(batch_count) == core)[:, None, None], residual_sum[None], 0.0
    ).reshape(tokens, model_width)
    kept, sent = combine(
        jnp.concatenate([gate_high, gate_low]), returned, kept_first(own_sum)
    )
    return (
        (kept + swap_cores(sent)).astype(jnp.bfloat16).reshape(batch_count, token_rows, model_width)
    )


def solution(mesh):
    chips = Mesh(mesh.devices.reshape(2, 4, 2, 4, 2), ("zl", "y", "zh", "x", "core"))
    expert = ("zh", "x", "core")
    every = CONTEXT + expert
    placed = (
        P(None, CONTEXT, expert),
        P(None, CONTEXT, None),
        P(None, CONTEXT, None),
        P(expert, None),
        P(None, every, None),
        P(),
        P(every, None, None),
        P(every, None, None),
        P(None, every, None),
        P(None, every, None),
    )
    return jax.shard_map(
        local,
        mesh=chips,
        in_specs=placed,
        out_specs=P(None, every, None),
        check_vma=False,
    )
```

```python
import functools

import jax
import jax.numpy as jnp
from jax import lax
from jax.experimental import pallas as pl
from jax.experimental.pallas import tpu as pltpu
from jax.sharding import Mesh, PartitionSpec as P

QH = 32
KVH = 4
HD = 128
BLOCK = 64
masked_score = -1e30

CONTEXT = ("zl", "y")
COLUMN = ("zh", "x")
CHIPS = ("zl", "y", "zh", "x")
SWAP = [(0, 1), (1, 0)]


def swap_cores(value):
    return lax.ppermute(value, "core", SWAP)


def folded(rows, piece, context_size):
    block_order = jnp.where(rows < BLOCK, piece, 2 * context_size - 1 - piece)
    return block_order * BLOCK + rows % BLOCK


def attention_kernel(
    index_ref, own_ref, other_ref, kv_ref, proj_ref, other_proj_ref, out_ref, proj, sems
):
    context_size, _, row_count, _ = kv_ref.shape
    feature_count = own_ref.shape[1]
    copies = [
        pltpu.make_async_copy(source, proj.at[pl.ds(part * feature_count, feature_count)], sems.at[part])
        for part, source in enumerate((proj_ref, other_proj_ref))
    ]
    for copy in copies:
        copy.start()
    key_count = context_size * row_count
    keys = kv_ref[:, 0].reshape(key_count, HD)
    values = kv_ref[:, 1].reshape(key_count, HD)
    query_rows = lax.broadcasted_iota(jnp.int32, (row_count, key_count), 0)
    key_rows = lax.broadcasted_iota(jnp.int32, (row_count, key_count), 1)
    allowed = folded(key_rows % row_count, key_rows // row_count, context_size) <= folded(
        query_rows, index_ref[0], context_size
    )
    heads = []
    for source in (own_ref, other_ref):
        for head in range(feature_count // HD):
            query = source[:, head * HD : (head + 1) * HD]
            scores = lax.dot_general(
                query, keys, (((1,), (1,)), ((), ())), preferred_element_type=jnp.float32
            ) * HD ** (-0.5)
            scores = jnp.where(allowed, scores, masked_score)
            weights = jnp.exp(scores - jnp.max(scores, axis=-1, keepdims=True))
            total = jnp.sum(weights, axis=-1, keepdims=True)
            weighted = jnp.dot(
                weights.astype(jnp.bfloat16), values, preferred_element_type=jnp.float32
            )
            heads.append((weighted / total).astype(jnp.bfloat16))
    attended = jnp.concatenate(heads, axis=1)
    for copy in copies:
        copy.wait()
    out_ref[...] = jnp.dot(attended, proj[...], preferred_element_type=jnp.float32).astype(
        jnp.bfloat16
    )


def attend(context_index, own, other, gathered, out_proj, other_proj):
    row_count, feature_count = own.shape
    model_width = out_proj.shape[1]
    whole = pl.BlockSpec(memory_space=pltpu.VMEM)
    apart = pl.BlockSpec(memory_space=pl.ANY)
    return pl.pallas_call(
        attention_kernel,
        in_specs=[pl.BlockSpec(memory_space=pltpu.SMEM), whole, whole, whole, apart, apart],
        out_specs=whole,
        out_shape=jax.ShapeDtypeStruct((row_count, model_width), jnp.bfloat16),
        scratch_shapes=[
            pltpu.VMEM((2 * feature_count, model_width), jnp.bfloat16),
            pltpu.SemaphoreType.DMA((2,)),
        ],
        compiler_params=pltpu.CompilerParams(vmem_limit_bytes=48 * 2**20),
    )(context_index, own, other, gathered, out_proj, other_proj)


def starts(sizes):
    return [sum(sizes[:part]) for part in range(len(sizes))]


def expert_kernel(*refs, depths, widths, part_widths):
    row_refs = refs[: len(part_widths)]
    w_in_ref, w_out_ref, out_ref = refs[len(part_widths) : len(part_widths) + 3]
    rows, w_in, w_out, mixed, hidden, result, row_sems, in_sems, out_sem, result_sems = refs[
        len(part_widths) + 3 :
    ]
    half_width = w_out_ref.shape[0]
    pieces = list(zip(starts(depths), depths))
    row_copies = []
    for part, (first, size) in enumerate(pieces):
        holder, base = [
            (ref, base) for ref, base in zip(row_refs, starts(part_widths)) if base <= first
        ][-1]
        row_copies.append(
            pltpu.make_async_copy(
                holder.at[:, pl.ds(first - base, size)],
                rows.at[:, pl.ds(first, size)],
                row_sems.at[part],
            )
        )
    in_copies = [
        pltpu.make_async_copy(
            w_in_ref.at[pl.ds(first, size)], w_in.at[pl.ds(first, size)], in_sems.at[part]
        )
        for part, (first, size) in enumerate(pieces)
    ]
    out_copy = pltpu.make_async_copy(w_out_ref, w_out, out_sem)
    for part in range(len(pieces)):
        row_copies[part].start()
        in_copies[part].start()
    out_copy.start()
    for part, (first, size) in enumerate(pieces):
        row_copies[part].wait()
        in_copies[part].wait()
        product = jnp.dot(
            rows[:, first : first + size],
            w_in[first : first + size, :],
            preferred_element_type=jnp.float32,
        )
        if part == 0:
            mixed[...] = product
        elif part < len(pieces) - 1:
            mixed[...] += product
        else:
            total = mixed[...] + product
            gate = total[:, :half_width]
            hidden[...] = (gate / (1.0 + jnp.exp(-gate)) * total[:, half_width:]).astype(
                jnp.bfloat16
            )
    out_copy.wait()
    result_copies = []
    for part, (first, size) in enumerate(zip(starts(widths), widths)):
        columns = pl.ds(first, size)
        result[:, columns] = jnp.dot(
            hidden[...], w_out[:, columns], preferred_element_type=jnp.float32
        ).astype(jnp.bfloat16)
        copy = pltpu.make_async_copy(
            result.at[:, columns], out_ref.at[:, columns], result_sems.at[part]
        )
        copy.start()
        result_copies.append(copy)
    for copy in result_copies:
        copy.wait()


def expert_rows(row_parts, w_in, w_out):
    row_count = row_parts[0].shape[0]
    half_width, model_width = w_out.shape
    depths = tuple(model_width * part // 16 for part in (2, 4, 5, 5))
    widths = (model_width // 8,) * 8
    apart = pl.BlockSpec(memory_space=pl.ANY)
    return pl.pallas_call(
        functools.partial(
            expert_kernel,
            depths=depths,
            widths=widths,
            part_widths=tuple(part.shape[1] for part in row_parts),
        ),
        in_specs=[apart] * (len(row_parts) + 2),
        out_specs=apart,
        out_shape=jax.ShapeDtypeStruct((row_count, model_width), jnp.bfloat16),
        scratch_shapes=[
            pltpu.VMEM((row_count, model_width), jnp.bfloat16),
            pltpu.VMEM((model_width, 2 * half_width), jnp.bfloat16),
            pltpu.VMEM((half_width, model_width), jnp.bfloat16),
            pltpu.VMEM((row_count, 2 * half_width), jnp.float32),
            pltpu.VMEM((row_count, half_width), jnp.bfloat16),
            pltpu.VMEM((row_count, model_width), jnp.bfloat16),
            pltpu.SemaphoreType.DMA((len(depths),)),
            pltpu.SemaphoreType.DMA((len(depths),)),
            pltpu.SemaphoreType.DMA,
            pltpu.SemaphoreType.DMA((len(widths),)),
        ],
        compiler_params=pltpu.CompilerParams(vmem_limit_bytes=52 * 2**20),
    )(*row_parts, w_in, w_out)


def combine_kernel(gates_ref, returned_ref, base_ref, kept_ref, sent_ref):
    token_count = base_ref.shape[0]
    summed = jnp.dot(gates_ref[...], returned_ref[...], preferred_element_type=jnp.float32)
    total = summed[:token_count] + summed[token_count:] + base_ref[...]
    kept_ref[...] = total[: token_count // 2]
    sent_ref[...] = total[token_count // 2 :]


def combine(gates, returned, base):
    slot_count, model_width = returned.shape
    token_count = base.shape[0]
    width = model_width // 4
    half = jax.ShapeDtypeStruct((token_count // 2, model_width), jnp.float32)
    columns = lambda rows: pl.BlockSpec((rows, width), lambda step: (0, step))
    return pl.pallas_call(
        combine_kernel,
        grid=(model_width // width,),
        in_specs=[
            pl.BlockSpec(gates.shape, lambda step: (0, 0)),
            columns(slot_count),
            columns(token_count),
        ],
        out_specs=[columns(token_count // 2), columns(token_count // 2)],
        out_shape=[half, half],
        compiler_params=pltpu.CompilerParams(vmem_limit_bytes=32 * 2**20),
    )(gates, returned, base)


def local(
    queries, keys, values, out_proj, residual, norm_gain, w_in, w_out, expert_ids, gate_weights
):
    batch_count, row_count, feature_count = queries.shape
    token_rows, top_count = expert_ids.shape[1:]
    model_width = out_proj.shape[1]
    context_size = lax.axis_size(CONTEXT)
    column_size = lax.axis_size(COLUMN)
    chip_count = context_size * column_size
    core = lax.axis_index("core")
    heads_here = feature_count // HD
    chip_rows = 2 * token_rows

    def of_batch(value, index):
        return lax.dynamic_index_in_dim(value, index, 0, keepdims=False)

    other_queries = swap_cores(of_batch(queries, 1 - core))
    other_proj = swap_cores(out_proj)
    other_residual = swap_cores(of_batch(residual, 1 - core))
    other_ids = swap_cores(expert_ids)
    other_gates = swap_cores(gate_weights)

    def in_core_order(own, other, axis):
        stacked = jnp.stack([own, other], axis=axis)
        flipped = jnp.stack([other, own], axis=axis)
        return jnp.where(core == 0, stacked, flipped)

    kv_head = lax.axis_index(COLUMN) * 2 * heads_here // (QH // KVH)
    pair = jnp.stack([of_batch(keys, core), of_batch(values, core)])
    pair = lax.dynamic_slice_in_dim(pair, kv_head * HD, HD, 2)
    gathered = lax.all_to_all(
        jnp.broadcast_to(pair[None], (context_size,) + pair.shape), CONTEXT, 0, 0
    )
    projected = attend(
        lax.axis_index(CONTEXT).astype(jnp.int32).reshape(1),
        of_batch(queries, core),
        other_queries,
        gathered,
        out_proj,
        other_proj,
    )
    pieces = lax.all_to_all(
        projected.reshape(column_size, chip_rows, model_width), COLUMN, 0, 0
    )
    residual_rows = in_core_order(of_batch(residual, core), other_residual, 0)
    residual_sum = residual_rows.reshape(chip_rows, model_width).astype(jnp.float32) + jnp.sum(
        pieces.astype(jnp.float32), axis=0
    )
    scale_rows = lax.rsqrt(jnp.mean(residual_sum * residual_sum, axis=-1, keepdims=True) + 1e-06)
    normed = (residual_sum * scale_rows * norm_gain).astype(jnp.bfloat16)
    tokens = batch_count * chip_rows
    all_normed = in_core_order(normed, swap_cores(normed), 0).reshape(tokens, model_width)

    ids = in_core_order(expert_ids, other_ids, 1)
    gates = in_core_order(gate_weights, other_gates, 1).reshape(tokens, top_count)
    experts_total = chip_count
    onehot = (
        ids.reshape(batch_count * 2, token_rows * top_count)[:, :, None]
        == jnp.arange(experts_total, dtype=jnp.int32)
    ).astype(jnp.int32)
    slot_index = jnp.sum((jnp.cumsum(onehot, axis=1) - onehot) * onehot, axis=2)
    flat = ids.reshape(batch_count * 2, token_rows * top_count)
    block_index = jnp.arange(batch_count * 2, dtype=jnp.int32)[:, None]
    slots = batch_count * 2 * 2
    target = jnp.where(
        flat % 2 == core, (flat // 2) * slots + block_index * 2 + slot_index, -1
    ).reshape(tokens, top_count)
    slot_rows = experts_total // 2 * slots
    matches = target[None] == jnp.arange(slot_rows, dtype=jnp.int32)[:, None, None]
    gate_matrix = jnp.sum(jnp.where(matches, gates[None], 0.0), axis=2)
    placing = jnp.any(matches, axis=2).astype(jnp.bfloat16)

    def both_halves(matrix):
        grouped = matrix.reshape(context_size // 2, 1, slot_rows // (context_size // 2), tokens)
        return jnp.broadcast_to(
            grouped, (grouped.shape[0], 2, grouped.shape[2], tokens)
        ).reshape(2 * slot_rows, tokens)

    def kept_first(value):
        grouped = value.reshape((batch_count, 2, token_rows) + value.shape[1:])
        ordered = jnp.stack(
            [
                lax.dynamic_index_in_dim(grouped, core, 1, keepdims=False),
                lax.dynamic_index_in_dim(grouped, 1 - core, 1, keepdims=False),
            ]
        )
        return ordered.reshape(value.shape)

    gate_rows = kept_first(both_halves(gate_matrix).T)
    gate_high = gate_rows.astype(jnp.bfloat16)
    gate_low = (gate_rows - gate_high.astype(jnp.float32)).astype(jnp.bfloat16)
    own_sum = jnp.where(
        (jnp.arange(batch_count) == core)[:, None, None], residual_sum[None], 0.0
    ).reshape(tokens, model_width)
    both_gates = jnp.concatenate([gate_high, gate_low])
    base = kept_first(own_sum)
    first_width = model_width // 8

    def exchange(rows):
        width = rows.shape[1]
        return lax.all_to_all(rows.reshape(chip_count, slots, width), CHIPS, 0, 0).reshape(
            chip_count * slots, width
        )

    def dispatch(placing_rows, columns):
        return exchange(
            jnp.dot(placing_rows, columns, preferred_element_type=jnp.float32).astype(jnp.bfloat16)
        )

    def experts_and_back(row_parts, w_in, w_out, both_gates, base):
        return combine(both_gates, exchange(expert_rows(row_parts, w_in, w_out)), base)

    def at_once(placing_rows, all_normed, *rest):
        return experts_and_back([dispatch(placing_rows, all_normed)], *rest)

    def in_two(placing_rows, all_normed, *rest):
        first = dispatch(placing_rows, all_normed[:, :first_width])
        columns, first = lax.optimization_barrier((all_normed[:, first_width:], first))
        return experts_and_back([first, dispatch(placing_rows, columns)], *rest)

    kept, sent = lax.cond(
        core == 0,
        at_once,
        in_two,
        both_halves(placing),
        all_normed,
        w_in[0],
        w_out[0],
        both_gates,
        base,
    )
    return (
        (kept + swap_cores(sent)).astype(jnp.bfloat16).reshape(batch_count, token_rows, model_width)
    )


def solution(mesh):
    chips = Mesh(mesh.devices.reshape(2, 4, 2, 4, 2), ("zl", "y", "zh", "x", "core"))
    expert = ("zh", "x", "core")
    every = CONTEXT + expert
    placed = (
        P(None, CONTEXT, expert),
        P(None, CONTEXT, None),
        P(None, CONTEXT, None),
        P(expert, None),
        P(None, every, None),
        P(),
        P(every, None, None),
        P(every, None, None),
        P(None, every, None),
        P(None, every, None),
    )
    return jax.shard_map(
        local,
        mesh=chips,
        in_specs=placed,
        out_specs=P(None, every, None),
        check_vma=False,
    )
```

```python
import jax
import jax.numpy as jnp
from jax import lax
from jax.experimental import pallas as pl
from jax.experimental.pallas import tpu as pltpu
from jax.sharding import Mesh, PartitionSpec as P

QH = 32
KVH = 4
HD = 128
BLOCK = 64
masked_score = -1e30

CONTEXT = ("zl", "y")
COLUMN = ("zh", "x")
CHIPS = ("zl", "y", "zh", "x")
SWAP = [(0, 1), (1, 0)]


def swap_cores(value):
    return lax.ppermute(value, "core", SWAP)


def folded(rows, piece, context_size):
    block_order = jnp.where(rows < BLOCK, piece, 2 * context_size - 1 - piece)
    return block_order * BLOCK + (rows & (BLOCK - 1))


def attention_kernel(
    index_ref, own_ref, other_ref, kv_ref, proj_ref, other_proj_ref, out_ref, proj, sems
):
    context_size, _, row_count, _ = kv_ref.shape
    feature_count = own_ref.shape[1]
    copies = [
        pltpu.make_async_copy(source, proj.at[pl.ds(part * feature_count, feature_count)], sems.at[part])
        for part, source in enumerate((proj_ref, other_proj_ref))
    ]
    for copy in copies:
        copy.start()
    key_count = context_size * row_count
    keys = kv_ref[:, 0].reshape(key_count, HD)
    values = kv_ref[:, 1].reshape(key_count, HD)
    query_rows = lax.broadcasted_iota(jnp.int32, (row_count, 1), 0)
    key_rows = lax.broadcasted_iota(jnp.int32, (1, key_count), 1)
    allowed = folded(key_rows % row_count, key_rows // row_count, context_size) <= folded(
        query_rows, index_ref[0], context_size
    )
    heads = []
    for source in (own_ref, other_ref):
        head_count = feature_count // HD
        query = jnp.concatenate(
            [source[:, head * HD : (head + 1) * HD] for head in range(head_count)], axis=0
        )
        scores = lax.dot_general(
            query, keys, (((1,), (1,)), ((), ())), preferred_element_type=jnp.float32
        ) * HD ** (-0.5)
        scores = jnp.where(
            allowed[None], scores.reshape(head_count, row_count, key_count), masked_score
        ).reshape(head_count * row_count, key_count)
        weights = jnp.exp(scores - jnp.max(scores, axis=-1, keepdims=True))
        total = jnp.sum(weights, axis=-1, keepdims=True)
        weighted = jnp.dot(
            weights.astype(jnp.bfloat16), values, preferred_element_type=jnp.float32
        )
        rows = (weighted / total).astype(jnp.bfloat16)
        heads += [rows[head * row_count : (head + 1) * row_count] for head in range(head_count)]
    attended = jnp.concatenate(heads, axis=1)
    for copy in copies:
        copy.wait()
    out_ref[...] = jnp.dot(attended, proj[...], preferred_element_type=jnp.float32).astype(
        jnp.bfloat16
    )


def attend(context_index, own, other, gathered, out_proj, other_proj):
    row_count, feature_count = own.shape
    model_width = out_proj.shape[1]
    whole = pl.BlockSpec(memory_space=pltpu.VMEM)
    apart = pl.BlockSpec(memory_space=pl.ANY)
    return pl.pallas_call(
        attention_kernel,
        in_specs=[pl.BlockSpec(memory_space=pltpu.SMEM), whole, whole, whole, apart, apart],
        out_specs=whole,
        out_shape=jax.ShapeDtypeStruct((row_count, model_width), jnp.bfloat16),
        scratch_shapes=[
            pltpu.VMEM((2 * feature_count, model_width), jnp.bfloat16),
            pltpu.SemaphoreType.DMA((2,)),
        ],
        compiler_params=pltpu.CompilerParams(vmem_limit_bytes=48 * 2**20),
    )(context_index, own, other, gathered, out_proj, other_proj)


def expert_rows(rows, w_in, w_out, started=None):
    half_width, model_width = w_out.shape
    mixed = jnp.dot(
        rows, w_in[model_width - rows.shape[1] :], preferred_element_type=jnp.float32
    )
    if started is not None:
        mixed = mixed + started
    hidden = (jax.nn.silu(mixed[:, :half_width]) * mixed[:, half_width:]).astype(jnp.bfloat16)
    return jnp.dot(hidden, w_out, preferred_element_type=jnp.float32).astype(jnp.bfloat16)


def combine_kernel(gates_ref, returned_ref, base_ref, kept_ref, sent_ref):
    token_count = base_ref.shape[0]
    summed = jnp.dot(gates_ref[...], returned_ref[...], preferred_element_type=jnp.float32)
    total = summed[:token_count] + summed[token_count:] + base_ref[...]
    kept_ref[...] = total[: token_count // 2]
    sent_ref[...] = total[token_count // 2 :]


def combine(gates, returned, base):
    slot_count, model_width = returned.shape
    token_count = base.shape[0]
    width = model_width // 4
    half = jax.ShapeDtypeStruct((token_count // 2, model_width), jnp.float32)
    columns = lambda rows: pl.BlockSpec((rows, width), lambda step: (0, step))
    return pl.pallas_call(
        combine_kernel,
        grid=(model_width // width,),
        in_specs=[
            pl.BlockSpec(gates.shape, lambda step: (0, 0)),
            columns(slot_count),
            columns(token_count),
        ],
        out_specs=[columns(token_count // 2), columns(token_count // 2)],
        out_shape=[half, half],
        compiler_params=pltpu.CompilerParams(vmem_limit_bytes=32 * 2**20),
    )(gates, returned, base)


def local(
    queries, keys, values, out_proj, residual, norm_gain, w_in, w_out, expert_ids, gate_weights
):
    batch_count, row_count, feature_count = queries.shape
    token_rows, top_count = expert_ids.shape[1:]
    model_width = out_proj.shape[1]
    context_size = lax.axis_size(CONTEXT)
    column_size = lax.axis_size(COLUMN)
    chip_count = context_size * column_size
    core = lax.axis_index("core")
    heads_here = feature_count // HD
    chip_rows = 2 * token_rows

    def of_batch(value, index):
        return lax.dynamic_index_in_dim(value, index, 0, keepdims=False)

    kv_head = lax.axis_index(COLUMN) * 2 * heads_here // (QH // KVH)
    pair = jnp.stack([of_batch(keys, core), of_batch(values, core)])
    pair = lax.dynamic_slice_in_dim(pair, kv_head * HD, HD, 2)
    spread = jnp.broadcast_to(pair[None], (context_size,) + pair.shape)
    spread, queries, out_proj, residual, expert_ids, gate_weights = lax.optimization_barrier(
        (spread, queries, out_proj, residual, expert_ids, gate_weights)
    )
    gathered = lax.all_to_all(spread, CONTEXT, 0, 0)
    other_queries = of_batch(swap_cores(queries), core)
    other_proj = swap_cores(out_proj)
    other_residual = of_batch(swap_cores(residual), core)
    other_ids = swap_cores(expert_ids)
    other_gates = swap_cores(gate_weights)

    def in_core_order(own, other, axis):
        stacked = jnp.stack([own, other], axis=axis)
        flipped = jnp.stack([other, own], axis=axis)
        return jnp.where(core == 0, stacked, flipped)

    projected = attend(
        lax.axis_index(CONTEXT).astype(jnp.int32).reshape(1),
        of_batch(queries, core),
        other_queries,
        gathered,
        out_proj,
        other_proj,
    )
    pieces = lax.all_to_all(
        projected.reshape(column_size, chip_rows, model_width), COLUMN, 0, 0
    )
    residual_rows = in_core_order(of_batch(residual, core), other_residual, 0)
    residual_sum = residual_rows.reshape(chip_rows, model_width).astype(jnp.float32) + jnp.sum(
        pieces.astype(jnp.float32), axis=0
    )
    scale_rows = lax.rsqrt(jnp.mean(residual_sum * residual_sum, axis=-1, keepdims=True) + 1e-06)
    normed = (residual_sum * scale_rows * norm_gain).astype(jnp.bfloat16)
    tokens = batch_count * chip_rows
    all_normed = in_core_order(normed, swap_cores(normed), 0).reshape(tokens, model_width)

    ids = in_core_order(expert_ids, other_ids, 1)
    gates = in_core_order(gate_weights, other_gates, 1).reshape(tokens, top_count)
    experts_total = chip_count
    onehot = (
        ids.reshape(batch_count * 2, token_rows * top_count)[:, :, None]
        == jnp.arange(experts_total, dtype=jnp.int32)
    ).astype(jnp.int32)
    slot_index = jnp.sum((jnp.cumsum(onehot, axis=1) - onehot) * onehot, axis=2)
    flat = ids.reshape(batch_count * 2, token_rows * top_count)
    block_index = jnp.arange(batch_count * 2, dtype=jnp.int32)[:, None]
    slots = batch_count * 2 * 2
    target = jnp.where(
        flat % 2 == core, (flat // 2) * slots + block_index * 2 + slot_index, -1
    ).reshape(tokens, top_count)
    slot_rows = experts_total // 2 * slots
    matches = target[None] == jnp.arange(slot_rows, dtype=jnp.int32)[:, None, None]
    gate_matrix = jnp.sum(jnp.where(matches, gates[None], 0.0), axis=2)
    placing = jnp.any(matches, axis=2).astype(jnp.bfloat16)

    def both_halves(matrix):
        grouped = matrix.reshape(context_size // 2, 1, slot_rows // (context_size // 2), tokens)
        return jnp.broadcast_to(
            grouped, (grouped.shape[0], 2, grouped.shape[2], tokens)
        ).reshape(2 * slot_rows, tokens)

    def kept_first(value):
        grouped = value.reshape((batch_count, 2, token_rows) + value.shape[1:])
        ordered = jnp.stack(
            [
                lax.dynamic_index_in_dim(grouped, core, 1, keepdims=False),
                lax.dynamic_index_in_dim(grouped, 1 - core, 1, keepdims=False),
            ]
        )
        return ordered.reshape(value.shape)

    gate_rows = kept_first(both_halves(gate_matrix).T)
    gate_high = gate_rows.astype(jnp.bfloat16)
    gate_low = (gate_rows - gate_high.astype(jnp.float32)).astype(jnp.bfloat16)
    own_sum = jnp.where(
        (jnp.arange(batch_count) == core)[:, None, None], residual_sum[None], 0.0
    ).reshape(tokens, model_width)
    both_gates = jnp.concatenate([gate_high, gate_low])
    base = kept_first(own_sum)
    first_width = 1024

    def exchange(rows):
        width = rows.shape[1]
        return lax.all_to_all(rows.reshape(chip_count, slots, width), CHIPS, 0, 0).reshape(
            chip_count * slots, width
        )

    def place(placing_rows, columns):
        return jnp.dot(placing_rows, columns, preferred_element_type=jnp.float32).astype(
            jnp.bfloat16
        )

    def at_once(placing_rows, all_normed, w_in, w_out, both_gates, base):
        partial_value = expert_rows(exchange(place(placing_rows, all_normed)), w_in, w_out)
        return combine(both_gates, exchange(partial_value), base)

    def in_two(placing_rows, all_normed, w_in, w_out, both_gates, base):
        first = exchange(place(placing_rows, all_normed[:, :first_width]))
        started = jnp.dot(first, w_in[:first_width], preferred_element_type=jnp.float32)
        outgoing, started = lax.optimization_barrier(
            (place(placing_rows, all_normed[:, first_width:]), started)
        )
        second = exchange(outgoing)
        partial_value = expert_rows(second, w_in, w_out, started)
        return combine(both_gates, exchange(partial_value), base)

    kept, sent = lax.cond(
        core == 0,
        at_once,
        in_two,
        both_halves(placing),
        all_normed,
        w_in[0],
        w_out[0],
        both_gates,
        base,
    )
    return (
        (kept + swap_cores(sent)).astype(jnp.bfloat16).reshape(batch_count, token_rows, model_width)
    )


def solution(mesh):
    chips = Mesh(mesh.devices.reshape(2, 4, 2, 4, 2), ("zl", "y", "zh", "x", "core"))
    expert = ("zh", "x", "core")
    every = CONTEXT + expert
    placed = (
        P(None, CONTEXT, expert),
        P(None, CONTEXT, None),
        P(None, CONTEXT, None),
        P(expert, None),
        P(None, every, None),
        P(),
        P(every, None, None),
        P(every, None, None),
        P(None, every, None),
        P(None, every, None),
    )
    return jax.shard_map(
        local,
        mesh=chips,
        in_specs=placed,
        out_specs=P(None, every, None),
        check_vma=False,
    )
```

```python
import jax
import jax.numpy as jnp
from jax import lax
from jax.experimental import pallas as pl
from jax.experimental.pallas import tpu as pltpu
from jax.sharding import Mesh, PartitionSpec as P

QH = 32
KVH = 4
HD = 128
BLOCK = 64
masked_score = -1e30

CONTEXT = ("zl", "y")
COLUMN = ("zh", "x")
CHIPS = ("zl", "y", "zh", "x")
SWAP = [(0, 1), (1, 0)]


def swap_cores(value):
    return lax.ppermute(value, "core", SWAP)


def folded(rows, piece, context_size):
    block_order = jnp.where(rows < BLOCK, piece, 2 * context_size - 1 - piece)
    return block_order * BLOCK + (rows & (BLOCK - 1))


def attention_kernel(
    index_ref, own_ref, other_ref, kv_ref, proj_ref, other_proj_ref, out_ref, proj, sems
):
    context_size, _, row_count, _ = kv_ref.shape
    feature_count = own_ref.shape[1]
    copies = [
        pltpu.make_async_copy(source, proj.at[pl.ds(part * feature_count, feature_count)], sems.at[part])
        for part, source in enumerate((proj_ref, other_proj_ref))
    ]
    for copy in copies:
        copy.start()
    key_count = context_size * row_count
    keys = kv_ref[:, 0].reshape(key_count, HD)
    values = kv_ref[:, 1].reshape(key_count, HD)
    query_rows = lax.broadcasted_iota(jnp.int32, (row_count, 1), 0)
    key_rows = lax.broadcasted_iota(jnp.int32, (1, key_count), 1)
    allowed = folded(key_rows % row_count, key_rows // row_count, context_size) <= folded(
        query_rows, index_ref[0], context_size
    )
    heads = []
    for source in (own_ref, other_ref):
        head_count = feature_count // HD
        query = jnp.concatenate(
            [source[:, head * HD : (head + 1) * HD] for head in range(head_count)], axis=0
        )
        scores = lax.dot_general(
            query, keys, (((1,), (1,)), ((), ())), preferred_element_type=jnp.float32
        ) * HD ** (-0.5)
        scores = jnp.where(
            allowed[None], scores.reshape(head_count, row_count, key_count), masked_score
        ).reshape(head_count * row_count, key_count)
        weights = jnp.exp(scores - jnp.max(scores, axis=-1, keepdims=True))
        total = jnp.sum(weights, axis=-1, keepdims=True)
        weighted = jnp.dot(
            weights.astype(jnp.bfloat16), values, preferred_element_type=jnp.float32
        )
        rows = (weighted / total).astype(jnp.bfloat16)
        heads += [rows[head * row_count : (head + 1) * row_count] for head in range(head_count)]
    attended = jnp.concatenate(heads, axis=1)
    for copy in copies:
        copy.wait()
    out_ref[...] = jnp.dot(attended, proj[...], preferred_element_type=jnp.float32).astype(
        jnp.bfloat16
    )


def attend(context_index, own, other, gathered, out_proj, other_proj):
    row_count, feature_count = own.shape
    model_width = out_proj.shape[1]
    whole = pl.BlockSpec(memory_space=pltpu.VMEM)
    apart = pl.BlockSpec(memory_space=pl.ANY)
    return pl.pallas_call(
        attention_kernel,
        in_specs=[pl.BlockSpec(memory_space=pltpu.SMEM), whole, whole, whole, apart, apart],
        out_specs=whole,
        out_shape=jax.ShapeDtypeStruct((row_count, model_width), jnp.bfloat16),
        scratch_shapes=[
            pltpu.VMEM((2 * feature_count, model_width), jnp.bfloat16),
            pltpu.SemaphoreType.DMA((2,)),
        ],
        compiler_params=pltpu.CompilerParams(vmem_limit_bytes=48 * 2**20),
    )(context_index, own, other, gathered, out_proj, other_proj)


def expert_rows(rows, w_in, w_out, started=None):
    half_width, model_width = w_out.shape
    mixed = jnp.dot(
        rows, w_in[model_width - rows.shape[1] :], preferred_element_type=jnp.float32
    )
    if started is not None:
        mixed = mixed + started
    hidden = (jax.nn.silu(mixed[:, :half_width]) * mixed[:, half_width:]).astype(jnp.bfloat16)
    return jnp.dot(hidden, w_out, preferred_element_type=jnp.float32).astype(jnp.bfloat16)


def combine_kernel(gates_ref, returned_ref, base_ref, kept_ref, sent_ref):
    token_count = base_ref.shape[0]
    summed = jnp.dot(gates_ref[...], returned_ref[...], preferred_element_type=jnp.float32)
    total = summed[:token_count] + summed[token_count:] + base_ref[...]
    kept_ref[...] = total[: token_count // 2]
    sent_ref[...] = total[token_count // 2 :].astype(sent_ref.dtype)


def combine(gates, returned, base):
    slot_count, model_width = returned.shape
    token_count = base.shape[0]
    width = model_width // 4
    half = (token_count // 2, model_width)
    columns = lambda rows: pl.BlockSpec((rows, width), lambda step: (0, step))
    return pl.pallas_call(
        combine_kernel,
        grid=(model_width // width,),
        in_specs=[
            pl.BlockSpec(gates.shape, lambda step: (0, 0)),
            columns(slot_count),
            columns(token_count),
        ],
        out_specs=[columns(token_count // 2), columns(token_count // 2)],
        out_shape=[
            jax.ShapeDtypeStruct(half, jnp.float32),
            jax.ShapeDtypeStruct(half, jnp.bfloat16),
        ],
        compiler_params=pltpu.CompilerParams(vmem_limit_bytes=32 * 2**20),
    )(gates, returned, base)


def local(
    queries, keys, values, out_proj, residual, norm_gain, w_in, w_out, expert_ids, gate_weights
):
    batch_count, row_count, feature_count = queries.shape
    token_rows, top_count = expert_ids.shape[1:]
    model_width = out_proj.shape[1]
    context_size = lax.axis_size(CONTEXT)
    column_size = lax.axis_size(COLUMN)
    chip_count = context_size * column_size
    core = lax.axis_index("core")
    heads_here = feature_count // HD
    chip_rows = 2 * token_rows

    def of_batch(value, index):
        return lax.dynamic_index_in_dim(value, index, 0, keepdims=False)

    kv_head = lax.axis_index(COLUMN) * 2 * heads_here // (QH // KVH)
    pair = jnp.concatenate(
        [
            lax.dynamic_slice(value, (core, 0, kv_head * HD), (1, row_count, HD))
            for value in (keys, values)
        ]
    )
    spread = jnp.broadcast_to(pair[None], (context_size,) + pair.shape)
    spread, queries, out_proj, residual, expert_ids, gate_weights = lax.optimization_barrier(
        (spread, queries, out_proj, residual, expert_ids, gate_weights)
    )
    gathered = lax.all_to_all(spread, CONTEXT, 0, 0)
    other_queries = of_batch(swap_cores(queries), core)
    other_proj = swap_cores(out_proj)
    other_residual = of_batch(swap_cores(residual), core)
    other_ids = swap_cores(expert_ids)
    other_gates = swap_cores(gate_weights)

    def in_core_order(own, other, axis):
        stacked = jnp.stack([own, other], axis=axis)
        flipped = jnp.stack([other, own], axis=axis)
        return jnp.where(core == 0, stacked, flipped)

    projected = attend(
        lax.axis_index(CONTEXT).astype(jnp.int32).reshape(1),
        of_batch(queries, core),
        other_queries,
        gathered,
        out_proj,
        other_proj,
    )
    pieces = lax.all_to_all(
        projected.reshape(column_size, chip_rows, model_width), COLUMN, 0, 0
    )
    residual_rows = in_core_order(of_batch(residual, core), other_residual, 0)
    residual_sum = residual_rows.reshape(chip_rows, model_width).astype(jnp.float32) + jnp.sum(
        pieces.astype(jnp.float32), axis=0
    )
    scale_rows = lax.rsqrt(jnp.mean(residual_sum * residual_sum, axis=-1, keepdims=True) + 1e-06)
    normed = (residual_sum * scale_rows * norm_gain).astype(jnp.bfloat16)
    tokens = batch_count * chip_rows
    all_normed = in_core_order(normed, swap_cores(normed), 0).reshape(tokens, model_width)

    ids = in_core_order(expert_ids, other_ids, 1)
    gates = in_core_order(gate_weights, other_gates, 1).reshape(tokens, top_count)
    experts_total = chip_count
    onehot = (
        ids.reshape(batch_count * 2, token_rows * top_count)[:, :, None]
        == jnp.arange(experts_total, dtype=jnp.int32)
    ).astype(jnp.int32)
    slot_index = jnp.sum((jnp.cumsum(onehot, axis=1) - onehot) * onehot, axis=2)
    flat = ids.reshape(batch_count * 2, token_rows * top_count)
    block_index = jnp.arange(batch_count * 2, dtype=jnp.int32)[:, None]
    slots = batch_count * 2 * 2
    target = jnp.where(
        flat % 2 == core, (flat // 2) * slots + block_index * 2 + slot_index, -1
    ).reshape(tokens, top_count)
    slot_rows = experts_total // 2 * slots
    matches = target[None] == jnp.arange(slot_rows, dtype=jnp.int32)[:, None, None]
    gate_matrix = jnp.sum(jnp.where(matches, gates[None], 0.0), axis=2)
    placing = jnp.any(matches, axis=2).astype(jnp.bfloat16)

    def both_halves(matrix):
        grouped = matrix.reshape(context_size // 2, 1, slot_rows // (context_size // 2), tokens)
        return jnp.broadcast_to(
            grouped, (grouped.shape[0], 2, grouped.shape[2], tokens)
        ).reshape(2 * slot_rows, tokens)

    def kept_first(value):
        grouped = value.reshape((batch_count, 2, token_rows) + value.shape[1:])
        ordered = jnp.stack(
            [
                lax.dynamic_index_in_dim(grouped, core, 1, keepdims=False),
                lax.dynamic_index_in_dim(grouped, 1 - core, 1, keepdims=False),
            ]
        )
        return ordered.reshape(value.shape)

    gate_rows = kept_first(both_halves(gate_matrix).T)
    gate_high = gate_rows.astype(jnp.bfloat16)
    gate_low = (gate_rows - gate_high.astype(jnp.float32)).astype(jnp.bfloat16)
    own_sum = jnp.where(
        (jnp.arange(batch_count) == core)[:, None, None], residual_sum[None], 0.0
    ).reshape(tokens, model_width)
    both_gates = jnp.concatenate([gate_high, gate_low])
    base = kept_first(own_sum)
    first_width = model_width // 4

    def exchange(rows):
        width = rows.shape[1]
        return lax.all_to_all(rows.reshape(chip_count, slots, width), CHIPS, 0, 0).reshape(
            chip_count * slots, width
        )

    def place(placing_rows, columns):
        return jnp.dot(placing_rows, columns, preferred_element_type=jnp.float32).astype(
            jnp.bfloat16
        )

    def at_once(placing_rows, all_normed, w_in, w_out, both_gates, base):
        partial_value = expert_rows(exchange(place(placing_rows, all_normed)), w_in, w_out)
        return combine(both_gates, exchange(partial_value), base)

    def in_two(placing_rows, all_normed, w_in, w_out, both_gates, base):
        first = exchange(place(placing_rows, all_normed[:, :first_width]))
        started = jnp.dot(first, w_in[:first_width], preferred_element_type=jnp.float32)
        outgoing, started = lax.optimization_barrier(
            (place(placing_rows, all_normed[:, first_width:]), started)
        )
        second = exchange(outgoing)
        partial_value = expert_rows(second, w_in, w_out, started)
        return combine(both_gates, exchange(partial_value), base)

    kept, sent = lax.cond(
        core == 0,
        at_once,
        in_two,
        both_halves(placing),
        all_normed,
        w_in[0],
        w_out[0],
        both_gates,
        base,
    )
    return (
        (kept + swap_cores(sent).astype(jnp.float32)).astype(jnp.bfloat16).reshape(batch_count, token_rows, model_width)
    )


def solution(mesh):
    chips = Mesh(mesh.devices.reshape(2, 4, 2, 4, 2), ("zl", "y", "zh", "x", "core"))
    expert = ("zh", "x", "core")
    every = CONTEXT + expert
    placed = (
        P(None, CONTEXT, expert),
        P(None, CONTEXT, None),
        P(None, CONTEXT, None),
        P(expert, None),
        P(None, every, None),
        P(),
        P(every, None, None),
        P(every, None, None),
        P(None, every, None),
        P(None, every, None),
    )
    return jax.shard_map(
        local,
        mesh=chips,
        in_specs=placed,
        out_specs=P(None, every, None),
        check_vma=False,
    )
```

```python
import jax
import jax.numpy as jnp
from jax import lax
from jax.experimental import pallas as pl
from jax.experimental.pallas import tpu as pltpu
from jax.sharding import Mesh, PartitionSpec as P

QH = 32
KVH = 4
HD = 128
BLOCK = 64
masked_score = -1e30

CONTEXT = ("zl", "y")
COLUMN = ("zh", "x")
CHIPS = ("zl", "y", "zh", "x")
SWAP = [(0, 1), (1, 0)]


def swap_cores(value):
    return lax.ppermute(value, "core", SWAP)


def folded(rows, piece, context_size):
    block_order = jnp.where(rows < BLOCK, piece, 2 * context_size - 1 - piece)
    return block_order * BLOCK + (rows & (BLOCK - 1))


def attention_kernel(
    index_ref, own_ref, other_ref, kv_ref, proj_ref, other_proj_ref, out_ref, proj, sems
):
    context_size, _, row_count, _ = kv_ref.shape
    feature_count = own_ref.shape[1]
    copies = [
        pltpu.make_async_copy(source, proj.at[pl.ds(part * feature_count, feature_count)], sems.at[part])
        for part, source in enumerate((proj_ref, other_proj_ref))
    ]
    for copy in copies:
        copy.start()
    key_count = context_size * row_count
    keys = kv_ref[:, 0].reshape(key_count, HD)
    values = kv_ref[:, 1].reshape(key_count, HD)
    query_rows = lax.broadcasted_iota(jnp.int32, (row_count, 1), 0)
    key_rows = lax.broadcasted_iota(jnp.int32, (1, key_count), 1)
    allowed = folded(key_rows % row_count, key_rows // row_count, context_size) <= folded(
        query_rows, index_ref[0], context_size
    )
    heads = []
    for source in (own_ref, other_ref):
        head_count = feature_count // HD
        query = jnp.concatenate(
            [source[:, head * HD : (head + 1) * HD] for head in range(head_count)], axis=0
        )
        scores = lax.dot_general(
            query, keys, (((1,), (1,)), ((), ())), preferred_element_type=jnp.float32
        ) * HD ** (-0.5)
        scores = jnp.where(
            allowed[None], scores.reshape(head_count, row_count, key_count), masked_score
        ).reshape(head_count * row_count, key_count)
        weights = jnp.exp(scores - jnp.max(scores, axis=-1, keepdims=True))
        total = jnp.sum(weights, axis=-1, keepdims=True)
        weighted = jnp.dot(
            weights.astype(jnp.bfloat16), values, preferred_element_type=jnp.float32
        )
        rows = (weighted / total).astype(jnp.bfloat16)
        heads += [rows[head * row_count : (head + 1) * row_count] for head in range(head_count)]
    attended = jnp.concatenate(heads, axis=1)
    for copy in copies:
        copy.wait()
    out_ref[...] = jnp.dot(attended, proj[...], preferred_element_type=jnp.float32).astype(
        jnp.bfloat16
    )


def attend(context_index, own, other, gathered, out_proj, other_proj):
    row_count, feature_count = own.shape
    model_width = out_proj.shape[1]
    whole = pl.BlockSpec(memory_space=pltpu.VMEM)
    apart = pl.BlockSpec(memory_space=pl.ANY)
    return pl.pallas_call(
        attention_kernel,
        in_specs=[pl.BlockSpec(memory_space=pltpu.SMEM), whole, whole, whole, apart, apart],
        out_specs=whole,
        out_shape=jax.ShapeDtypeStruct((row_count, model_width), jnp.bfloat16),
        scratch_shapes=[
            pltpu.VMEM((2 * feature_count, model_width), jnp.bfloat16),
            pltpu.SemaphoreType.DMA((2,)),
        ],
        compiler_params=pltpu.CompilerParams(vmem_limit_bytes=48 * 2**20),
    )(context_index, own, other, gathered, out_proj, other_proj)


def expert_rows(rows, w_in, w_out, started=None):
    half_width, model_width = w_out.shape
    mixed = jnp.dot(
        rows, w_in[model_width - rows.shape[1] :], preferred_element_type=jnp.float32
    )
    if started is not None:
        mixed = mixed + started
    hidden = (jax.nn.silu(mixed[:, :half_width]) * mixed[:, half_width:]).astype(jnp.bfloat16)
    return jnp.dot(hidden, w_out, preferred_element_type=jnp.float32).astype(jnp.bfloat16)


def combine_kernel(core_ref, gates_ref, returned_ref, residual_ref, kept_ref, sent_ref):
    chip_rows = residual_ref.shape[0]
    token_rows = chip_rows // 2
    token_count = gates_ref.shape[0] // 2
    summed = jnp.dot(gates_ref[...], returned_ref[...], preferred_element_type=jnp.float32)
    total = summed[:token_count] + summed[token_count:]
    first, second = residual_ref[:token_rows], residual_ref[token_rows:]
    on_first = core_ref[0] == 0
    own = (jnp.where(on_first, first, second), jnp.where(on_first, second, first))
    for out_ref, rows, part in ((kept_ref, own[0], 0), (sent_ref, own[1], 1)):
        for batch in range(2):
            start = part * chip_rows + batch * token_rows
            mine = on_first if batch == 0 else jnp.logical_not(on_first)
            out_ref[batch * token_rows : (batch + 1) * token_rows] = (
                total[start : start + token_rows] + jnp.where(mine, rows, 0.0)
            ).astype(out_ref.dtype)


def combine(core, gates, returned, residual_sum):
    model_width = returned.shape[1]
    half = (gates.shape[0] // 4, model_width)
    whole = pl.BlockSpec(memory_space=pltpu.VMEM)
    return pl.pallas_call(
        combine_kernel,
        in_specs=[pl.BlockSpec(memory_space=pltpu.SMEM), whole, whole, whole],
        out_specs=[whole, whole],
        out_shape=[
            jax.ShapeDtypeStruct(half, jnp.float32),
            jax.ShapeDtypeStruct(half, jnp.bfloat16),
        ],
        compiler_params=pltpu.CompilerParams(vmem_limit_bytes=24 * 2**20),
    )(core.astype(jnp.int32).reshape(1), gates, returned, residual_sum)


def local(
    queries, keys, values, out_proj, residual, norm_gain, w_in, w_out, expert_ids, gate_weights
):
    batch_count, row_count, feature_count = queries.shape
    token_rows, top_count = expert_ids.shape[1:]
    model_width = out_proj.shape[1]
    context_size = lax.axis_size(CONTEXT)
    column_size = lax.axis_size(COLUMN)
    chip_count = context_size * column_size
    core = lax.axis_index("core")
    heads_here = feature_count // HD
    chip_rows = 2 * token_rows

    def of_batch(value, index):
        return lax.dynamic_index_in_dim(value, index, 0, keepdims=False)

    kv_head = lax.axis_index(COLUMN) * 2 * heads_here // (QH // KVH)
    pair = jnp.concatenate(
        [
            lax.dynamic_slice(value, (core, 0, kv_head * HD), (1, row_count, HD))
            for value in (keys, values)
        ]
    )
    spread = jnp.broadcast_to(pair[None], (context_size,) + pair.shape)
    spread, queries, out_proj, residual, expert_ids, gate_weights = lax.optimization_barrier(
        (spread, queries, out_proj, residual, expert_ids, gate_weights)
    )
    gathered = lax.all_to_all(spread, CONTEXT, 0, 0)
    other_queries = of_batch(swap_cores(queries), core)
    other_proj = swap_cores(out_proj)
    other_residual = of_batch(swap_cores(residual), core)
    other_ids = swap_cores(expert_ids)
    other_gates = swap_cores(gate_weights)

    def in_core_order(own, other, axis):
        stacked = jnp.stack([own, other], axis=axis)
        flipped = jnp.stack([other, own], axis=axis)
        return jnp.where(core == 0, stacked, flipped)

    projected = attend(
        lax.axis_index(CONTEXT).astype(jnp.int32).reshape(1),
        of_batch(queries, core),
        other_queries,
        gathered,
        out_proj,
        other_proj,
    )
    pieces = lax.all_to_all(
        projected.reshape(column_size, chip_rows, model_width), COLUMN, 0, 0
    )
    residual_rows = in_core_order(of_batch(residual, core), other_residual, 0)
    residual_sum = residual_rows.reshape(chip_rows, model_width).astype(jnp.float32) + jnp.sum(
        pieces.astype(jnp.float32), axis=0
    )
    scale_rows = lax.rsqrt(jnp.mean(residual_sum * residual_sum, axis=-1, keepdims=True) + 1e-06)
    normed = (residual_sum * scale_rows * norm_gain).astype(jnp.bfloat16)
    tokens = batch_count * chip_rows
    all_normed = in_core_order(normed, swap_cores(normed), 0).reshape(tokens, model_width)

    ids = in_core_order(expert_ids, other_ids, 1)
    gates = in_core_order(gate_weights, other_gates, 1).reshape(tokens, top_count)
    experts_total = chip_count
    onehot = (
        ids.reshape(batch_count * 2, token_rows * top_count)[:, :, None]
        == jnp.arange(experts_total, dtype=jnp.int32)
    ).astype(jnp.int32)
    slot_index = jnp.sum((jnp.cumsum(onehot, axis=1) - onehot) * onehot, axis=2)
    flat = ids.reshape(batch_count * 2, token_rows * top_count)
    block_index = jnp.arange(batch_count * 2, dtype=jnp.int32)[:, None]
    slots = batch_count * 2 * 2
    target = jnp.where(
        flat % 2 == core, (flat // 2) * slots + block_index * 2 + slot_index, -1
    ).reshape(tokens, top_count)
    slot_rows = experts_total // 2 * slots
    matches = target[None] == jnp.arange(slot_rows, dtype=jnp.int32)[:, None, None]
    gate_matrix = jnp.sum(jnp.where(matches, gates[None], 0.0), axis=2)
    placing = jnp.any(matches, axis=2).astype(jnp.bfloat16)

    def both_halves(matrix):
        grouped = matrix.reshape(context_size // 2, 1, slot_rows // (context_size // 2), tokens)
        return jnp.broadcast_to(
            grouped, (grouped.shape[0], 2, grouped.shape[2], tokens)
        ).reshape(2 * slot_rows, tokens)

    def kept_first(value):
        grouped = value.reshape((batch_count, 2, token_rows) + value.shape[1:])
        ordered = jnp.stack(
            [
                lax.dynamic_index_in_dim(grouped, core, 1, keepdims=False),
                lax.dynamic_index_in_dim(grouped, 1 - core, 1, keepdims=False),
            ]
        )
        return ordered.reshape(value.shape)

    gate_rows = kept_first(both_halves(gate_matrix).T)
    gate_high = gate_rows.astype(jnp.bfloat16)
    gate_low = (gate_rows - gate_high.astype(jnp.float32)).astype(jnp.bfloat16)
    both_gates = jnp.concatenate([gate_high, gate_low])
    first_width = model_width // 4

    def exchange(rows):
        width = rows.shape[1]
        return lax.all_to_all(rows.reshape(chip_count, slots, width), CHIPS, 0, 0).reshape(
            chip_count * slots, width
        )

    def place(placing_rows, columns):
        return jnp.dot(placing_rows, columns, preferred_element_type=jnp.float32).astype(
            jnp.bfloat16
        )

    def at_once(placing_rows, all_normed, w_in, w_out, both_gates, residual_sum):
        partial_value = expert_rows(exchange(place(placing_rows, all_normed)), w_in, w_out)
        return combine(core, both_gates, exchange(partial_value), residual_sum)

    def in_two(placing_rows, all_normed, w_in, w_out, both_gates, residual_sum):
        first = exchange(place(placing_rows, all_normed[:, :first_width]))
        started = jnp.dot(
            first, w_in[:first_width], preferred_element_type=jnp.float32
        ).astype(jnp.bfloat16)
        columns, started = lax.optimization_barrier((all_normed[:, first_width:], started))
        second = exchange(place(placing_rows, columns))
        partial_value = expert_rows(second, w_in, w_out, started)
        return combine(core, both_gates, exchange(partial_value), residual_sum)

    kept, sent = lax.cond(
        core == 0,
        at_once,
        in_two,
        both_halves(placing),
        all_normed,
        w_in[0],
        w_out[0],
        both_gates,
        residual_sum,
    )
    return (
        (kept + swap_cores(sent).astype(jnp.float32)).astype(jnp.bfloat16).reshape(batch_count, token_rows, model_width)
    )


def solution(mesh):
    chips = Mesh(mesh.devices.reshape(2, 4, 2, 4, 2), ("zl", "y", "zh", "x", "core"))
    expert = ("zh", "x", "core")
    every = CONTEXT + expert
    placed = (
        P(None, CONTEXT, expert),
        P(None, CONTEXT, None),
        P(None, CONTEXT, None),
        P(expert, None),
        P(None, every, None),
        P(),
        P(every, None, None),
        P(every, None, None),
        P(None, every, None),
        P(None, every, None),
    )
    return jax.shard_map(
        local,
        mesh=chips,
        in_specs=placed,
        out_specs=P(None, every, None),
        check_vma=False,
    )
```

```python
import jax
import jax.numpy as jnp
from jax import lax
from jax.experimental import pallas as pl
from jax.experimental.pallas import tpu as pltpu
from jax.sharding import Mesh, PartitionSpec as P

QH = 32
KVH = 4
HD = 128
BLOCK = 64
masked_score = -1e30

CONTEXT = ("zl", "y")
COLUMN = ("zh", "x")
CHIPS = ("zl", "y", "zh", "x")
SWAP = [(0, 1), (1, 0)]


def swap_cores(value):
    return lax.ppermute(value, "core", SWAP)


def folded(rows, piece, context_size):
    block_order = jnp.where(rows < BLOCK, piece, 2 * context_size - 1 - piece)
    return block_order * BLOCK + (rows & (BLOCK - 1))


def attention_kernel(
    index_ref, own_ref, other_ref, kv_ref, proj_ref, other_proj_ref, out_ref, proj, sems
):
    context_size, _, row_count, _ = kv_ref.shape
    feature_count = own_ref.shape[1]
    copies = [
        pltpu.make_async_copy(source, proj.at[pl.ds(part * feature_count, feature_count)], sems.at[part])
        for part, source in enumerate((proj_ref, other_proj_ref))
    ]
    for copy in copies:
        copy.start()
    key_count = context_size * row_count
    keys = kv_ref[:, 0].reshape(key_count, HD)
    values = kv_ref[:, 1].reshape(key_count, HD)
    query_rows = lax.broadcasted_iota(jnp.int32, (row_count, 1), 0)
    key_rows = lax.broadcasted_iota(jnp.int32, (1, key_count), 1)
    allowed = folded(key_rows % row_count, key_rows // row_count, context_size) <= folded(
        query_rows, index_ref[0], context_size
    )
    heads = []
    for source in (own_ref, other_ref):
        head_count = feature_count // HD
        query = jnp.concatenate(
            [source[:, head * HD : (head + 1) * HD] for head in range(head_count)], axis=0
        )
        scores = lax.dot_general(
            query, keys, (((1,), (1,)), ((), ())), preferred_element_type=jnp.float32
        ) * HD ** (-0.5)
        scores = jnp.where(
            allowed[None], scores.reshape(head_count, row_count, key_count), masked_score
        ).reshape(head_count * row_count, key_count)
        weights = jnp.exp(scores - jnp.max(scores, axis=-1, keepdims=True))
        total = jnp.sum(weights, axis=-1, keepdims=True)
        weighted = jnp.dot(
            weights.astype(jnp.bfloat16), values, preferred_element_type=jnp.float32
        )
        rows = (weighted / total).astype(jnp.bfloat16)
        heads += [rows[head * row_count : (head + 1) * row_count] for head in range(head_count)]
    attended = jnp.concatenate(heads, axis=1)
    for copy in copies:
        copy.wait()
    out_ref[...] = jnp.dot(attended, proj[...], preferred_element_type=jnp.float32).astype(
        jnp.bfloat16
    )


def attend(context_index, own, other, gathered, out_proj, other_proj):
    row_count, feature_count = own.shape
    model_width = out_proj.shape[1]
    whole = pl.BlockSpec(memory_space=pltpu.VMEM)
    apart = pl.BlockSpec(memory_space=pl.ANY)
    return pl.pallas_call(
        attention_kernel,
        in_specs=[pl.BlockSpec(memory_space=pltpu.SMEM), whole, whole, whole, apart, apart],
        out_specs=whole,
        out_shape=jax.ShapeDtypeStruct((row_count, model_width), jnp.bfloat16),
        scratch_shapes=[
            pltpu.VMEM((2 * feature_count, model_width), jnp.bfloat16),
            pltpu.SemaphoreType.DMA((2,)),
        ],
        compiler_params=pltpu.CompilerParams(vmem_limit_bytes=48 * 2**20),
    )(context_index, own, other, gathered, out_proj, other_proj)


def expert_rows(rows, w_in, w_out, started=None):
    half_width, model_width = w_out.shape
    mixed = jnp.dot(
        rows, w_in[model_width - rows.shape[1] :], preferred_element_type=jnp.float32
    )
    if started is not None:
        mixed = mixed + started
    hidden = (jax.nn.silu(mixed[:, :half_width]) * mixed[:, half_width:]).astype(jnp.bfloat16)
    return jnp.dot(hidden, w_out, preferred_element_type=jnp.float32).astype(jnp.bfloat16)


def combine_kernel(core_ref, gates_ref, returned_ref, residual_ref, kept_ref, sent_ref):
    chip_rows = residual_ref.shape[0]
    token_rows = chip_rows // 2
    token_count = gates_ref.shape[0] // 2
    summed = jnp.dot(gates_ref[...], returned_ref[...], preferred_element_type=jnp.float32)
    total = summed[:token_count] + summed[token_count:]
    first, second = residual_ref[:token_rows], residual_ref[token_rows:]
    on_first = core_ref[0] == 0
    own = (jnp.where(on_first, first, second), jnp.where(on_first, second, first))
    for out_ref, rows, start in ((kept_ref, own[0], 0), (sent_ref, own[1], chip_rows)):
        added = jnp.concatenate(
            [jnp.where(on_first, rows, 0.0), jnp.where(on_first, 0.0, rows)], axis=0
        )
        out_ref[...] = (total[start : start + chip_rows] + added).astype(out_ref.dtype)


def combine(core, gates, returned, residual_sum):
    model_width = returned.shape[1]
    half = (gates.shape[0] // 4, model_width)
    whole = pl.BlockSpec(memory_space=pltpu.VMEM)
    return pl.pallas_call(
        combine_kernel,
        in_specs=[pl.BlockSpec(memory_space=pltpu.SMEM), whole, whole, whole],
        out_specs=[whole, whole],
        out_shape=[
            jax.ShapeDtypeStruct(half, jnp.float32),
            jax.ShapeDtypeStruct(half, jnp.bfloat16),
        ],
        compiler_params=pltpu.CompilerParams(vmem_limit_bytes=24 * 2**20),
    )(core.astype(jnp.int32).reshape(1), gates, returned, residual_sum)


def local(
    queries, keys, values, out_proj, residual, norm_gain, w_in, w_out, expert_ids, gate_weights
):
    batch_count, row_count, feature_count = queries.shape
    token_rows, top_count = expert_ids.shape[1:]
    model_width = out_proj.shape[1]
    context_size = lax.axis_size(CONTEXT)
    column_size = lax.axis_size(COLUMN)
    chip_count = context_size * column_size
    core = lax.axis_index("core")
    heads_here = feature_count // HD
    chip_rows = 2 * token_rows

    def of_batch(value, index):
        return lax.dynamic_index_in_dim(value, index, 0, keepdims=False)

    kv_head = lax.axis_index(COLUMN) * 2 * heads_here // (QH // KVH)
    pair = jnp.concatenate(
        [
            lax.dynamic_slice(value, (core, 0, kv_head * HD), (1, row_count, HD))
            for value in (keys, values)
        ]
    )
    spread = jnp.broadcast_to(pair[None], (context_size,) + pair.shape)
    spread, queries, out_proj, residual, expert_ids, gate_weights = lax.optimization_barrier(
        (spread, queries, out_proj, residual, expert_ids, gate_weights)
    )
    gathered = lax.all_to_all(spread, CONTEXT, 0, 0)
    other_queries = of_batch(swap_cores(queries), core)
    other_proj = swap_cores(out_proj)
    other_residual = of_batch(swap_cores(residual), core)
    other_ids = swap_cores(expert_ids)
    other_gates = swap_cores(gate_weights)

    def in_core_order(own, other, axis):
        stacked = jnp.stack([own, other], axis=axis)
        flipped = jnp.stack([other, own], axis=axis)
        return jnp.where(core == 0, stacked, flipped)

    projected = attend(
        lax.axis_index(CONTEXT).astype(jnp.int32).reshape(1),
        of_batch(queries, core),
        other_queries,
        gathered,
        out_proj,
        other_proj,
    )
    pieces = lax.all_to_all(
        projected.reshape(column_size, chip_rows, model_width), COLUMN, 0, 0
    )
    residual_rows = in_core_order(of_batch(residual, core), other_residual, 0)
    residual_sum = residual_rows.reshape(chip_rows, model_width).astype(jnp.float32) + jnp.sum(
        pieces.astype(jnp.float32), axis=0
    )
    scale_rows = lax.rsqrt(jnp.mean(residual_sum * residual_sum, axis=-1, keepdims=True) + 1e-06)
    normed = (residual_sum * scale_rows * norm_gain).astype(jnp.bfloat16)
    tokens = batch_count * chip_rows
    all_normed = in_core_order(normed, swap_cores(normed), 0).reshape(tokens, model_width)

    ids = in_core_order(expert_ids, other_ids, 1)
    gates = in_core_order(gate_weights, other_gates, 1).reshape(tokens, top_count)
    experts_total = chip_count
    onehot = (
        ids.reshape(batch_count * 2, token_rows * top_count)[:, :, None]
        == jnp.arange(experts_total, dtype=jnp.int32)
    ).astype(jnp.int32)
    slot_index = jnp.sum((jnp.cumsum(onehot, axis=1) - onehot) * onehot, axis=2)
    flat = ids.reshape(batch_count * 2, token_rows * top_count)
    block_index = jnp.arange(batch_count * 2, dtype=jnp.int32)[:, None]
    slots = batch_count * 2 * 2
    target = jnp.where(
        flat % 2 == core, (flat // 2) * slots + block_index * 2 + slot_index, -1
    ).reshape(tokens, top_count)
    slot_rows = experts_total // 2 * slots
    matches = target[None] == jnp.arange(slot_rows, dtype=jnp.int32)[:, None, None]
    gate_matrix = jnp.sum(jnp.where(matches, gates[None], 0.0), axis=2)
    placing = jnp.any(matches, axis=2).astype(jnp.bfloat16)

    def both_halves(matrix):
        grouped = matrix.reshape(context_size // 2, 1, slot_rows // (context_size // 2), tokens)
        return jnp.broadcast_to(
            grouped, (grouped.shape[0], 2, grouped.shape[2], tokens)
        ).reshape(2 * slot_rows, tokens)

    def kept_first(value):
        grouped = value.reshape((batch_count, 2, token_rows) + value.shape[1:])
        ordered = jnp.stack(
            [
                lax.dynamic_index_in_dim(grouped, core, 1, keepdims=False),
                lax.dynamic_index_in_dim(grouped, 1 - core, 1, keepdims=False),
            ]
        )
        return ordered.reshape(value.shape)

    gate_rows = kept_first(both_halves(gate_matrix).T)
    gate_high = gate_rows.astype(jnp.bfloat16)
    gate_low = (gate_rows - gate_high.astype(jnp.float32)).astype(jnp.bfloat16)
    both_gates = jnp.concatenate([gate_high, gate_low])
    first_width = model_width // 4

    def exchange(rows):
        width = rows.shape[1]
        return lax.all_to_all(rows.reshape(chip_count, slots, width), CHIPS, 0, 0).reshape(
            chip_count * slots, width
        )

    def place(placing_rows, columns):
        return jnp.dot(placing_rows, columns, preferred_element_type=jnp.float32).astype(
            jnp.bfloat16
        )

    def at_once(placing_rows, all_normed, w_in, w_out, both_gates, residual_sum):
        partial_value = expert_rows(exchange(place(placing_rows, all_normed)), w_in, w_out)
        return combine(core, both_gates, exchange(partial_value), residual_sum)

    def in_two(placing_rows, all_normed, w_in, w_out, both_gates, residual_sum):
        first = exchange(place(placing_rows, all_normed[:, :first_width]))
        started = jnp.dot(
            first, w_in[:first_width], preferred_element_type=jnp.float32
        ).astype(jnp.bfloat16)
        columns, started = lax.optimization_barrier((all_normed[:, first_width:], started))
        second = exchange(place(placing_rows, columns))
        partial_value = expert_rows(second, w_in, w_out, started)
        return combine(core, both_gates, exchange(partial_value), residual_sum)

    kept, sent = lax.cond(
        core == 0,
        at_once,
        in_two,
        both_halves(placing),
        all_normed,
        w_in[0],
        w_out[0],
        both_gates,
        residual_sum,
    )
    return (
        (kept + swap_cores(sent).astype(jnp.float32)).astype(jnp.bfloat16).reshape(batch_count, token_rows, model_width)
    )


def solution(mesh):
    chips = Mesh(mesh.devices.reshape(2, 4, 2, 4, 2), ("zl", "y", "zh", "x", "core"))
    expert = ("zh", "x", "core")
    every = CONTEXT + expert
    placed = (
        P(None, CONTEXT, expert),
        P(None, CONTEXT, None),
        P(None, CONTEXT, None),
        P(expert, None),
        P(None, every, None),
        P(),
        P(every, None, None),
        P(every, None, None),
        P(None, every, None),
        P(None, every, None),
    )
    return jax.shard_map(
        local,
        mesh=chips,
        in_specs=placed,
        out_specs=P(None, every, None),
        check_vma=False,
    )
```

```python
import jax
import jax.numpy as jnp
from jax import lax
from jax.experimental import pallas as pl
from jax.experimental.pallas import tpu as pltpu
from jax.sharding import Mesh, PartitionSpec as P

QH = 32
KVH = 4
HD = 128
BLOCK = 64
masked_score = -1e30

CONTEXT = ("zl", "y")
COLUMN = ("zh", "x")
CHIPS = ("zl", "y", "zh", "x")
SWAP = [(0, 1), (1, 0)]


def swap_cores(value):
    return lax.ppermute(value, "core", SWAP)


def folded(rows, piece, context_size):
    block_order = jnp.where(rows < BLOCK, piece, 2 * context_size - 1 - piece)
    return block_order * BLOCK + (rows & (BLOCK - 1))


def attention_kernel(
    index_ref, own_ref, other_ref, kv_ref, proj_ref, other_proj_ref, out_ref, proj, sems
):
    context_size, _, row_count, _ = kv_ref.shape
    feature_count = own_ref.shape[1]
    copies = [
        pltpu.make_async_copy(source, proj.at[pl.ds(part * feature_count, feature_count)], sems.at[part])
        for part, source in enumerate((proj_ref, other_proj_ref))
    ]
    for copy in copies:
        copy.start()
    key_count = context_size * row_count
    keys = kv_ref[:, 0].reshape(key_count, HD)
    values = kv_ref[:, 1].reshape(key_count, HD)
    query_rows = lax.broadcasted_iota(jnp.int32, (row_count, 1), 0)
    key_rows = lax.broadcasted_iota(jnp.int32, (1, key_count), 1)
    allowed = folded(key_rows % row_count, key_rows // row_count, context_size) <= folded(
        query_rows, index_ref[0], context_size
    )
    projected = 0.0
    for part, source in enumerate((own_ref, other_ref)):
        head_count = feature_count // HD
        query = jnp.concatenate(
            [source[:, head * HD : (head + 1) * HD] for head in range(head_count)], axis=0
        )
        scores = lax.dot_general(
            query, keys, (((1,), (1,)), ((), ())), preferred_element_type=jnp.float32
        ) * HD ** (-0.5)
        scores = jnp.where(
            allowed[None], scores.reshape(head_count, row_count, key_count), masked_score
        ).reshape(head_count * row_count, key_count)
        weights = jnp.exp(scores - jnp.max(scores, axis=-1, keepdims=True))
        total = jnp.sum(weights, axis=-1, keepdims=True)
        weighted = jnp.dot(
            weights.astype(jnp.bfloat16), values, preferred_element_type=jnp.float32
        )
        rows = (weighted / total).astype(jnp.bfloat16)
        attended = jnp.concatenate(
            [rows[head * row_count : (head + 1) * row_count] for head in range(head_count)], axis=1
        )
        copies[part].wait()
        projected += jnp.dot(
            attended,
            proj[part * feature_count : (part + 1) * feature_count],
            preferred_element_type=jnp.float32,
        )
    out_ref[...] = projected.astype(jnp.bfloat16)


def attend(context_index, own, other, gathered, out_proj, other_proj):
    row_count, feature_count = own.shape
    model_width = out_proj.shape[1]
    whole = pl.BlockSpec(memory_space=pltpu.VMEM)
    apart = pl.BlockSpec(memory_space=pl.ANY)
    return pl.pallas_call(
        attention_kernel,
        in_specs=[pl.BlockSpec(memory_space=pltpu.SMEM), whole, whole, whole, apart, apart],
        out_specs=whole,
        out_shape=jax.ShapeDtypeStruct((row_count, model_width), jnp.bfloat16),
        scratch_shapes=[
            pltpu.VMEM((2 * feature_count, model_width), jnp.bfloat16),
            pltpu.SemaphoreType.DMA((2,)),
        ],
        compiler_params=pltpu.CompilerParams(vmem_limit_bytes=48 * 2**20),
    )(context_index, own, other, gathered, out_proj, other_proj)


def expert_rows(rows, w_in, w_out, started=None):
    half_width, model_width = w_out.shape
    mixed = jnp.dot(
        rows, w_in[model_width - rows.shape[1] :], preferred_element_type=jnp.float32
    )
    if started is not None:
        mixed = mixed + started
    hidden = (jax.nn.silu(mixed[:, :half_width]) * mixed[:, half_width:]).astype(jnp.bfloat16)
    return jnp.dot(hidden, w_out, preferred_element_type=jnp.float32).astype(jnp.bfloat16)


def combine_kernel(core_ref, gates_ref, returned_ref, residual_ref, kept_ref, sent_ref):
    chip_rows = residual_ref.shape[0]
    token_rows = chip_rows // 2
    token_count = gates_ref.shape[0] // 2
    summed = jnp.dot(gates_ref[...], returned_ref[...], preferred_element_type=jnp.float32)
    total = summed[:token_count] + summed[token_count:]
    first, second = residual_ref[:token_rows], residual_ref[token_rows:]
    on_first = core_ref[0] == 0
    own = (jnp.where(on_first, first, second), jnp.where(on_first, second, first))
    for out_ref, rows, start in ((kept_ref, own[0], 0), (sent_ref, own[1], chip_rows)):
        added = jnp.concatenate(
            [jnp.where(on_first, rows, 0.0), jnp.where(on_first, 0.0, rows)], axis=0
        )
        out_ref[...] = (total[start : start + chip_rows] + added).astype(out_ref.dtype)


def combine(core, gates, returned, residual_sum):
    model_width = returned.shape[1]
    half = (gates.shape[0] // 4, model_width)
    whole = pl.BlockSpec(memory_space=pltpu.VMEM)
    return pl.pallas_call(
        combine_kernel,
        in_specs=[pl.BlockSpec(memory_space=pltpu.SMEM), whole, whole, whole],
        out_specs=[whole, whole],
        out_shape=[
            jax.ShapeDtypeStruct(half, jnp.float32),
            jax.ShapeDtypeStruct(half, jnp.bfloat16),
        ],
        compiler_params=pltpu.CompilerParams(vmem_limit_bytes=24 * 2**20),
    )(core.astype(jnp.int32).reshape(1), gates, returned, residual_sum)


def local(
    queries, keys, values, out_proj, residual, norm_gain, w_in, w_out, expert_ids, gate_weights
):
    batch_count, row_count, feature_count = queries.shape
    token_rows, top_count = expert_ids.shape[1:]
    model_width = out_proj.shape[1]
    context_size = lax.axis_size(CONTEXT)
    column_size = lax.axis_size(COLUMN)
    chip_count = context_size * column_size
    core = lax.axis_index("core")
    heads_here = feature_count // HD
    chip_rows = 2 * token_rows

    def of_batch(value, index):
        return lax.dynamic_index_in_dim(value, index, 0, keepdims=False)

    kv_head = lax.axis_index(COLUMN) * 2 * heads_here // (QH // KVH)
    pair = jnp.concatenate(
        [
            lax.dynamic_slice(value, (core, 0, kv_head * HD), (1, row_count, HD))
            for value in (keys, values)
        ]
    )
    spread = jnp.broadcast_to(pair[None], (context_size,) + pair.shape)
    spread, queries, out_proj, residual, expert_ids, gate_weights = lax.optimization_barrier(
        (spread, queries, out_proj, residual, expert_ids, gate_weights)
    )
    gathered = lax.all_to_all(spread, CONTEXT, 0, 0)
    other_queries = of_batch(swap_cores(queries), core)
    other_proj = swap_cores(out_proj)
    other_residual = of_batch(swap_cores(residual), core)
    other_ids = swap_cores(expert_ids)
    other_gates = swap_cores(gate_weights)

    def in_core_order(own, other, axis):
        stacked = jnp.stack([own, other], axis=axis)
        flipped = jnp.stack([other, own], axis=axis)
        return jnp.where(core == 0, stacked, flipped)

    projected = attend(
        lax.axis_index(CONTEXT).astype(jnp.int32).reshape(1),
        of_batch(queries, core),
        other_queries,
        gathered,
        out_proj,
        other_proj,
    )
    pieces = lax.all_to_all(
        projected.reshape(column_size, chip_rows, model_width), COLUMN, 0, 0
    )
    residual_rows = in_core_order(of_batch(residual, core), other_residual, 0)
    residual_sum = residual_rows.reshape(chip_rows, model_width).astype(jnp.float32) + jnp.sum(
        pieces.astype(jnp.float32), axis=0
    )
    scale_rows = lax.rsqrt(jnp.mean(residual_sum * residual_sum, axis=-1, keepdims=True) + 1e-06)
    normed = (residual_sum * scale_rows * norm_gain).astype(jnp.bfloat16)
    tokens = batch_count * chip_rows
    all_normed = in_core_order(normed, swap_cores(normed), 0).reshape(tokens, model_width)

    ids = in_core_order(expert_ids, other_ids, 1)
    gates = in_core_order(gate_weights, other_gates, 1).reshape(tokens, top_count)
    experts_total = chip_count
    onehot = (
        ids.reshape(batch_count * 2, token_rows * top_count)[:, :, None]
        == jnp.arange(experts_total, dtype=jnp.int32)
    ).astype(jnp.int32)
    slot_index = jnp.sum((jnp.cumsum(onehot, axis=1) - onehot) * onehot, axis=2)
    flat = ids.reshape(batch_count * 2, token_rows * top_count)
    block_index = jnp.arange(batch_count * 2, dtype=jnp.int32)[:, None]
    slots = batch_count * 2 * 2
    target = jnp.where(
        flat % 2 == core, (flat // 2) * slots + block_index * 2 + slot_index, -1
    ).reshape(tokens, top_count)
    slot_rows = experts_total // 2 * slots
    matches = target[None] == jnp.arange(slot_rows, dtype=jnp.int32)[:, None, None]
    gate_matrix = jnp.sum(jnp.where(matches, gates[None], 0.0), axis=2)
    placing = jnp.any(matches, axis=2).astype(jnp.bfloat16)

    def both_halves(matrix):
        grouped = matrix.reshape(context_size // 2, 1, slot_rows // (context_size // 2), tokens)
        return jnp.broadcast_to(
            grouped, (grouped.shape[0], 2, grouped.shape[2], tokens)
        ).reshape(2 * slot_rows, tokens)

    def kept_first(value):
        grouped = value.reshape((batch_count, 2, token_rows) + value.shape[1:])
        ordered = jnp.stack(
            [
                lax.dynamic_index_in_dim(grouped, core, 1, keepdims=False),
                lax.dynamic_index_in_dim(grouped, 1 - core, 1, keepdims=False),
            ]
        )
        return ordered.reshape(value.shape)

    gate_rows = kept_first(both_halves(gate_matrix).T)
    gate_high = gate_rows.astype(jnp.bfloat16)
    gate_low = (gate_rows - gate_high.astype(jnp.float32)).astype(jnp.bfloat16)
    both_gates = jnp.concatenate([gate_high, gate_low])
    first_width = model_width // 4

    def exchange(rows):
        width = rows.shape[1]
        return lax.all_to_all(rows.reshape(chip_count, slots, width), CHIPS, 0, 0).reshape(
            chip_count * slots, width
        )

    def place(placing_rows, columns):
        return jnp.dot(placing_rows, columns, preferred_element_type=jnp.float32).astype(
            jnp.bfloat16
        )

    def at_once(placing_rows, all_normed, w_in, w_out, both_gates, residual_sum):
        partial_value = expert_rows(exchange(place(placing_rows, all_normed)), w_in, w_out)
        return combine(core, both_gates, exchange(partial_value), residual_sum)

    def in_two(placing_rows, all_normed, w_in, w_out, both_gates, residual_sum):
        first = exchange(place(placing_rows, all_normed[:, :first_width]))
        started = jnp.dot(
            first, w_in[:first_width], preferred_element_type=jnp.float32
        ).astype(jnp.bfloat16)
        columns, started = lax.optimization_barrier((all_normed[:, first_width:], started))
        second = exchange(place(placing_rows, columns))
        partial_value = expert_rows(second, w_in, w_out, started)
        return combine(core, both_gates, exchange(partial_value), residual_sum)

    kept, sent = lax.cond(
        core == 0,
        at_once,
        in_two,
        both_halves(placing),
        all_normed,
        w_in[0],
        w_out[0],
        both_gates,
        residual_sum,
    )
    return (
        (kept + swap_cores(sent).astype(jnp.float32)).astype(jnp.bfloat16).reshape(batch_count, token_rows, model_width)
    )


def solution(mesh):
    chips = Mesh(mesh.devices.reshape(2, 4, 2, 4, 2), ("zl", "y", "zh", "x", "core"))
    expert = ("zh", "x", "core")
    every = CONTEXT + expert
    placed = (
        P(None, CONTEXT, expert),
        P(None, CONTEXT, None),
        P(None, CONTEXT, None),
        P(expert, None),
        P(None, every, None),
        P(),
        P(every, None, None),
        P(every, None, None),
        P(None, every, None),
        P(None, every, None),
    )
    return jax.shard_map(
        local,
        mesh=chips,
        in_specs=placed,
        out_specs=P(None, every, None),
        check_vma=False,
    )
```
